256 devices in a mesh: cuts: 8 (over x_hi, y), mode: 32 (over z, x_lo, core).
Axes of the slice: x: 4 (x_hi: 2, x_lo: 2; x = x_hi * 2 + x_lo), y: 4, z: 8, core: 2. Of those that a mesh axis runs over, the one named last changes fastest.
Arguments:
- stem_tensor: bfloat16 [2, 32, 32, 32, 32, 256], P(None, 'cuts', 'mode'), may hold values from -6 to 6
- branch_first: bfloat16 [2, 32, 256, 256], P(None, 'cuts'), may hold values from -0.25 to 0.25
- branch_second: bfloat16 [2, 32, 512, 512], P(None, 'cuts', 'mode'), may hold values from -0.25 to 0.25
Outputs:
- amplitudes: float32 [2, 512, 32, 512], P(None, 'cuts', 'mode')
The draws below stay inside these ranges and needn't reach their ends.
All inputs are finite; a program needn't handle non-finite values.
Results may differ from the reference program's by a relative error of at most 0.0029.
Values may be sent and summed in bfloat16 or wider, within the bound.
No kernel may reach another device: no remote copies, remote signals or barrier semaphores. Data moves between devices by JAX's collectives and lax.ppermute only.
A program may use at most 64 MiB of HBM per device.

```python
import jax
import jax.numpy as jnp
from jax import lax

C = 256
G2 = 16
QB = 32
S = 32
P_SIZE = 32
QA = 32
GL = 16
K2 = 512
M = 512


def strengthened(entries, rng, source, target, parts, factor):
    def block_of(dim):
        return (jnp.arange(entries.shape[dim]) // (entries.shape[dim] // parts)).reshape((-1,) + (1,) * (entries.ndim - 1 - dim))

    one_side = jax.random.permutation(rng, parts)[block_of(target)]
    second = (block_of(target) + parts // 2) % parts
    return jnp.where((block_of(source) == one_side) | (block_of(source) == second), factor * entries, entries)


def steps_of(rng, dims, split, low, top_value):
    factor_of = 1.0
    for axis_at, blocks in split:
        heights = jax.random.uniform(jax.random.fold_in(jax.random.fold_in(rng, 6), axis_at), (blocks,), jnp.float32, low / len(split), top_value / len(split))
        factor_of = factor_of * jnp.repeat(jnp.exp(heights), dims[axis_at] // blocks).reshape((-1,) + (1,) * (len(dims) - 1 - axis_at))
    return factor_of


def centred(key, dims, width, limit, shards=(), held_as=jnp.bfloat16):
    values = jax.random.normal(key, dims, jnp.float32) * width
    if len(shards) > 0:
        values = steps_of(key, dims, shards, -0.22, 0.18) * values
    return jnp.clip(values, min=-limit, max=limit).astype(held_as)


def bell_draw_with(own_key, extent, deviation, limit, cuts, heavy, dtype=jnp.bfloat16):
    result = deviation * jax.random.normal(own_key, extent, jnp.float32)
    if cuts:
        result = result * steps_of(own_key, extent, cuts, -0.22, 0.18)
    return jnp.clip(strengthened(result, jax.random.fold_in(own_key, 3), *heavy), -limit, limit).astype(dtype)


def setup_inputs(seed: int = 0) -> dict:
    key_list = jax.random.split(jax.random.key(seed), 4)
    stem_tensor = centred(key_list[0], (2, S, P_SIZE, QA, QB, C), 1.0, 6.0, ((1, 8), (2, 32)))
    branch_first = centred(key_list[1], (2, S, C, C), (2 * C) ** -0.5, 0.25, ((1, 8),))
    branch_second = bell_draw_with(key_list[2], (2, S, K2, K2), (2 * K2) ** -0.5, 0.25, ((1, 8), (2, 32)), (1, 3, 8, 2.0))
    return dict(stem_tensor=stem_tensor, branch_first=branch_first, branch_second=branch_second)


def complex_first(block, branch):
    stem_real = block[0].astype(jnp.float32)
    stem_imag = block[1].astype(jnp.float32)
    br_real = branch[0].astype(jnp.float32)
    br_imag = branch[1].astype(jnp.float32)
    real_part = jnp.einsum('pabc,co->paob', stem_real, br_real) - jnp.einsum('pabc,co->paob', stem_imag, br_imag)
    imag_part = jnp.einsum('pabc,co->paob', stem_real, br_imag) + jnp.einsum('pabc,co->paob', stem_imag, br_real)
    return jnp.stack([real_part, imag_part]).astype(jnp.bfloat16)


def reference(stem_tensor, branch_first, branch_second):
    def one_slice(total, pieces):
        block, first_branch, second_branch = pieces
        first = complex_first(block, first_branch)
        regrouped = first.reshape(2, P_SIZE, QA, G2, GL, QB).transpose(0, 2, 1, 3, 4, 5).reshape(2, QA, K2, M)
        left_real = regrouped[0].astype(jnp.float32)
        left_imag = regrouped[1].astype(jnp.float32)
        br_real = second_branch[0].astype(jnp.float32)
        br_imag = second_branch[1].astype(jnp.float32)
        real_part = jnp.einsum('kj,akm->jam', br_real, left_real) - jnp.einsum('kj,akm->jam', br_imag, left_imag)
        imag_part = jnp.einsum('kj,akm->jam', br_imag, left_real) + jnp.einsum('kj,akm->jam', br_real, left_imag)
        return total + jnp.stack([real_part, imag_part]), None

    start = jnp.zeros((2, K2, QA, M), jnp.float32)
    pieces = (jnp.moveaxis(stem_tensor, 1, 0), jnp.moveaxis(branch_first, 1, 0), jnp.moveaxis(branch_second, 1, 0))
    total, unused = lax.scan(one_slice, start, pieces)
    return total
```

```python
import jax
import jax.numpy as jnp
from jax import lax
from jax.experimental import pallas as pl
from jax.experimental.pallas import tpu as pltpu
from jax.sharding import Mesh
from jax.sharding import PartitionSpec as P

PLANE = ("xh", "y", "xl", "core")
OWNERS = ("z", "xh", "y")
NT = (((1,), (1,)), ((), ()))
TN = (((0,), (0,)), ((), ()))


def first_kernel(stem_ref, branch_ref, out_ref):
    row = lax.broadcasted_iota(jnp.int32, (256, 256), 0)
    col = lax.broadcasted_iota(jnp.int32, (256, 256), 1)
    regroup = (col == (row % 16) * 16 + row // 16).astype(jnp.bfloat16)
    br = [
        lax.dot_general(regroup, branch_ref[r, 0], NT, preferred_element_type=jnp.float32).astype(jnp.bfloat16)
        for r in range(2)
    ]
    lhs = jnp.concatenate(
        [jnp.concatenate([br[0], -br[1]], axis=1), jnp.concatenate([br[1], br[0]], axis=1)], axis=0
    )
    for w in range(4):
        rhs = jnp.concatenate([stem_ref[r, 0, :, w].reshape(256, 256) for r in range(2)], axis=1)
        res = lax.dot_general(lhs, rhs, NT, preferred_element_type=jnp.float32).astype(jnp.bfloat16)
        for r in range(2):
            out_ref[:, w, r, 0] = res[r * 256 : (r + 1) * 256].reshape(8, 2, 16, 256)


def first_step(stem, branch):
    slices = stem.shape[1]
    return pl.pallas_call(
        first_kernel,
        grid=(slices,),
        in_specs=[
            pl.BlockSpec((2, 1, 8, 4, 32, 256), lambda s: (0, s, 0, 0, 0, 0)),
            pl.BlockSpec((2, 1, 256, 256), lambda s: (0, s, 0, 0)),
        ],
        out_specs=pl.BlockSpec((8, 4, 2, 1, 2, 16, 256), lambda s: (0, 0, 0, s, 0, 0, 0)),
        out_shape=jax.ShapeDtypeStruct((8, 4, 2, slices, 2, 16, 256), jnp.bfloat16),
        compiler_params=pltpu.CompilerParams(vmem_limit_bytes=32 << 20),
        cost_estimate=pl.CostEstimate(flops=2400000000, bytes_accessed=9 << 20, transcendentals=0),
        name="first_step",
    )(stem, branch)


def second_kernel(x_ref, b_ref, out_ref):
    br = [b_ref[:, r].reshape(2048, 128) for r in range(2)]
    lhs = [jnp.concatenate([br[0], -br[1]], axis=0), jnp.concatenate([br[1], br[0]], axis=0)]
    parts = []
    rhs = []
    for lh in range(2):
        rhs.append(jnp.concatenate([x_ref[:, r, :, lh].reshape(2048, 256) for r in range(2)], axis=0))
    for r in range(2):
        for lh in range(2):
            parts.append(lax.dot_general(lhs[r], rhs[lh], TN, preferred_element_type=jnp.float32))
    for za in range(8):
        joined = jnp.concatenate([part[:, za * 32 : (za + 1) * 32] for part in parts], axis=1)
        out_ref[za] = joined.astype(jnp.bfloat16).reshape(2, 64, 128)


def second_step(x, b2):
    return pl.pallas_call(
        second_kernel,
        grid=(4,),
        in_specs=[
            pl.BlockSpec((32, 2, 4, 2, 16, 256), lambda t: (0, 0, 0, 0, 0, 0)),
            pl.BlockSpec((32, 2, 4, 16, 128), lambda t: (0, 0, 0, 0, t)),
        ],
        out_specs=pl.BlockSpec((8, 2, 64, 128), lambda t: (0, t, 0, 0)),
        out_shape=jax.ShapeDtypeStruct((8, 8, 64, 128), jnp.bfloat16),
        compiler_params=pltpu.CompilerParams(vmem_limit_bytes=48 << 20),
        cost_estimate=pl.CostEstimate(flops=4300000000, bytes_accessed=9 << 20, transcendentals=0),
        name="second_step",
    )(x, b2)


def total_kernel(in_ref, out_ref):
    sums = []
    for i in range(8):
        acc = in_ref[0, i].astype(jnp.float32)
        for z in range(1, 8):
            acc = acc + in_ref[z, i].astype(jnp.float32)
        sums.append(acc)
    for r in range(2):
        out_ref[r] = jnp.concatenate([acc[:, r * 64 : (r + 1) * 64] for acc in sums], axis=1)


def total_step(arrived):
    return pl.pallas_call(
        total_kernel,
        out_shape=jax.ShapeDtypeStruct((2, 64, 512), jnp.float32),
        compiler_params=pltpu.CompilerParams(vmem_limit_bytes=16 << 20),
        cost_estimate=pl.CostEstimate(flops=1000000, bytes_accessed=2 << 20, transcendentals=0),
        name="total_step",
    )(arrived)


def shards(stem_tensor, branch_first, branch_second):
    slices = stem_tensor.shape[1]
    stem = stem_tensor.reshape(2, slices, 8, 4, 32, 256)
    b2 = lax.all_gather(branch_second.reshape(2 * slices * 16, 512), PLANE, axis=0, tiled=False)
    b2 = b2.reshape(32, 2, slices, 16, 512)
    sent = first_step(stem, branch_first).reshape(32, 2 * slices * 2 * 16, 256)
    arrived = lax.all_to_all(sent, PLANE, split_axis=0, concat_axis=0, tiled=True)
    partial = second_step(arrived.reshape(32, 2, slices, 2, 16, 256), b2)
    owned = lax.all_to_all(partial.reshape(64, 64, 128), OWNERS, split_axis=0, concat_axis=0, tiled=True)
    out = total_step(owned.reshape(8, 8, 64, 128))
    return out.reshape(2, 64, 1, 512)


def solution(mesh):
    fine = Mesh(mesh.devices.reshape(2, 4, 8, 2, 2), ("xh", "y", "z", "xl", "core"))
    cuts, mode = ("xh", "y"), ("z", "xl", "core")
    in_specs = (
        P(None, cuts, mode, None, None, None),
        P(None, cuts, None, None),
        P(None, cuts, mode, None),
    )
    return jax.shard_map(
        shards, mesh=fine, in_specs=in_specs, out_specs=P(None, cuts, mode, None), check_vma=False
    )
```

```python
import jax
import jax.numpy as jnp
from jax import lax
from jax.experimental import pallas as pl
from jax.experimental.pallas import tpu as pltpu
from jax.sharding import Mesh
from jax.sharding import PartitionSpec as P

PLANE = ("xh", "y", "xl", "core")
ROWS = ("xh", "xl")
OWNERS = ("xh", "y", "z")
NT = (((1,), (1,)), ((), ()))
NN = (((1,), (0,)), ((), ()))
RING = 4


def first_kernel(stem_ref, branch_ref, out_ref):
    row = lax.broadcasted_iota(jnp.int32, (256, 256), 0)
    col = lax.broadcasted_iota(jnp.int32, (256, 256), 1)
    regroup = (col == (row % 16) * 16 + row // 16).astype(jnp.bfloat16)
    br = [
        lax.dot_general(regroup, branch_ref[r, 0], NT, preferred_element_type=jnp.float32).astype(jnp.bfloat16)
        for r in range(2)
    ]
    lhs = jnp.concatenate(
        [jnp.concatenate([br[0], -br[1]], axis=1), jnp.concatenate([br[1], br[0]], axis=1)], axis=0
    )
    for w in range(4):
        rhs = jnp.concatenate([stem_ref[r, 0, :, w].reshape(256, 256) for r in range(2)], axis=1)
        res = lax.dot_general(lhs, rhs, NT, preferred_element_type=jnp.float32).astype(jnp.bfloat16)
        for r in range(2):
            out_ref[:, w, r, 0] = res[r * 256 : (r + 1) * 256].reshape(8, 2, 16, 256)


def first_step(stem, branch):
    slices = stem.shape[1]
    return pl.pallas_call(
        first_kernel,
        grid=(slices,),
        in_specs=[
            pl.BlockSpec((2, 1, 8, 4, 32, 256), lambda s: (0, s, 0, 0, 0, 0)),
            pl.BlockSpec((2, 1, 256, 256), lambda s: (0, s, 0, 0)),
        ],
        out_specs=pl.BlockSpec((8, 4, 2, 1, 2, 16, 256), lambda s: (0, 0, 0, s, 0, 0, 0)),
        out_shape=jax.ShapeDtypeStruct((8, 4, 2, slices, 2, 16, 256), jnp.bfloat16),
        compiler_params=pltpu.CompilerParams(vmem_limit_bytes=60 << 20),
        cost_estimate=pl.CostEstimate(flops=2400000000, bytes_accessed=9 << 20, transcendentals=0),
        name="first_step",
    )(stem, branch)


def turn_kernel(own_a, own_b, other_a, other_b, out_ref):
    for dx in range(RING):
        for dy in range(RING):
            at = (dx * RING + dy) * 128
            for r in range(2):
                a = jnp.concatenate([own_a[dx, dy, r], other_a[dx, dy, r]], axis=0)
                b = jnp.concatenate([own_b[dy, dx, r], other_b[dy, dx, r]], axis=0)
                out_ref[r, 0:256, at : at + 128] = a.T
                out_ref[r, 256:512, at : at + 128] = b.T


def turn_step(own_a, own_b, other_a, other_b):
    return pl.pallas_call(
        turn_kernel,
        out_shape=jax.ShapeDtypeStruct((2, 512, 2048), jnp.bfloat16),
        compiler_params=pltpu.CompilerParams(vmem_limit_bytes=32 << 20),
        cost_estimate=pl.CostEstimate(flops=4000000000, bytes_accessed=8 << 20, transcendentals=0),
        name="turn_step",
    )(own_a, own_b, other_a, other_b)


def second_kernel(me_ref, x_ref, b_ref, out_ref):
    lhs = [
        jnp.concatenate([b_ref[0], -b_ref[1]], axis=1),
        jnp.concatenate([b_ref[1], b_ref[0]], axis=1),
    ]
    rhs = []
    for lh in range(2):
        pieces = []
        for r in range(2):
            for dx in range(RING):
                x = (me_ref[0] + dx) % RING
                for dy in range(RING):
                    y = (me_ref[1] + dy) % RING
                    for dc in range(2):
                        c = (me_ref[2] + dc) % 2
                        pieces.append(x_ref[x // 2, y, x % 2, c, r, :, lh].reshape(64, 256))
        rhs.append(jnp.concatenate(pieces, axis=0))
    parts = []
    for r in range(2):
        for lh in range(2):
            parts.append(lax.dot_general(lhs[r], rhs[lh], NN, preferred_element_type=jnp.float32))
    for za in range(8):
        joined = jnp.concatenate([part[:, za * 32 : (za + 1) * 32] for part in parts], axis=1)
        out_ref[:, za] = joined.astype(jnp.bfloat16).reshape(2, 64, 128)


def second_step(me, x, b2):
    return pl.pallas_call(
        second_kernel,
        grid_spec=pltpu.PrefetchScalarGridSpec(
            num_scalar_prefetch=1,
            grid=(4,),
            in_specs=[
                pl.BlockSpec((2, 4, 2, 2, 2, 4, 2, 16, 256), lambda t, me: (0,) * 9),
                pl.BlockSpec((2, 128, 2048), lambda t, me: (0, t, 0)),
            ],
            out_specs=pl.BlockSpec((2, 8, 64, 128), lambda t, me: (t, 0, 0, 0)),
        ),
        out_shape=jax.ShapeDtypeStruct((8, 8, 64, 128), jnp.bfloat16),
        compiler_params=pltpu.CompilerParams(vmem_limit_bytes=60 << 20),
        cost_estimate=pl.CostEstimate(flops=4300000000, bytes_accessed=9 << 20, transcendentals=0),
        name="second_step",
    )(me, x, b2)


def total_kernel(in_ref, out_ref):
    sums = []
    for i in range(8):
        acc = in_ref[i, 0].astype(jnp.float32)
        for z in range(1, 8):
            acc = acc + in_ref[i, z].astype(jnp.float32)
        sums.append(acc)
    for r in range(2):
        out_ref[r] = jnp.concatenate([acc[:, r * 64 : (r + 1) * 64] for acc in sums], axis=1)


def total_step(arrived):
    return pl.pallas_call(
        total_kernel,
        out_shape=jax.ShapeDtypeStruct((2, 64, 512), jnp.float32),
        compiler_params=pltpu.CompilerParams(vmem_limit_bytes=16 << 20),
        cost_estimate=pl.CostEstimate(flops=1000000, bytes_accessed=2 << 20, transcendentals=0),
        name="total_step",
    )(arrived)


def ring_gather(block, axis):
    blocks = [block]
    for d in range(1, RING):
        blocks.append(lax.ppermute(block, axis, [(i, (i - d) % RING) for i in range(RING)]))
    return jnp.concatenate(blocks, axis=0)


def shards(stem_tensor, branch_first, branch_second):
    slices = stem_tensor.shape[1]
    stem = stem_tensor.reshape(2, slices, 8, 4, 32, 256)
    b2 = branch_second.reshape(1, 2, slices * 16, 512)
    half_a, half_b = ring_gather(b2[..., :256], "y"), ring_gather(b2[..., 256:], ROWS)
    sent = first_step(stem, branch_first).reshape(32, 2 * slices * 2 * 16, 256)
    arrived = lax.all_to_all(sent, PLANE, split_axis=0, concat_axis=0, tiled=True)
    half_a, half_b = ring_gather(half_a, ROWS), ring_gather(half_b, "y")
    swap = [(0, 1), (1, 0)]
    other_a, other_b = lax.ppermute(half_a, "core", swap), lax.ppermute(half_b, "core", swap)
    grid = (RING, RING, 2, slices * 16, 256)
    turned = turn_step(*(half.reshape(grid) for half in (half_a, half_b, other_a, other_b)))
    me = jnp.stack([lax.axis_index(ROWS), lax.axis_index("y"), lax.axis_index("core")]).astype(jnp.int32)
    partial = second_step(me, arrived.reshape(2, 4, 2, 2, 2, slices, 2, 16, 256), turned)
    owned = lax.all_to_all(partial.reshape(64, 64, 128), OWNERS, split_axis=0, concat_axis=0, tiled=True)
    out = total_step(owned.reshape(8, 8, 64, 128))
    return out.reshape(2, 64, 1, 512)


def solution(mesh):
    fine = Mesh(mesh.devices.reshape(2, 4, 8, 2, 2), ("xh", "y", "z", "xl", "core"))
    cuts, mode = ("xh", "y"), ("z", "xl", "core")
    in_specs = (
        P(None, cuts, mode, None, None, None),
        P(None, cuts, None, None),
        P(None, cuts, mode, None),
    )
    return jax.shard_map(
        shards, mesh=fine, in_specs=in_specs, out_specs=P(None, cuts, mode, None), check_vma=False
    )
```

```python
import functools

import jax
import jax.numpy as jnp
from jax import lax
from jax.experimental import pallas as pl
from jax.experimental.pallas import tpu as pltpu
from jax.sharding import Mesh
from jax.sharding import PartitionSpec as P

PLANE = ("xh", "y", "xl", "core")
ROWS = ("xh", "xl")
OWNERS = ("z", "xh", "y")
NT = (((1,), (1,)), ((), ()))
NN = (((1,), (0,)), ((), ()))
RING = 4


def first_kernel(begin, count, stem_hbm, branch_hbm, *refs):
    out_hbm, stem, branch, lhs, out, in_sem, branch_sem, out_sem = refs[-8:]
    part = pl.ds(begin, count)
    branch_copy = pltpu.make_async_copy(branch_hbm.at[:, part], branch, branch_sem)
    branch_copy.start()
    copies = [
        pltpu.make_async_copy(stem_hbm.at[:, part, :, w], stem.at[:, :, :, w], in_sem.at[w]) for w in range(4)
    ]
    for copy in copies:
        copy.start()
    row = lax.broadcasted_iota(jnp.int32, (256, 256), 0)
    col = lax.broadcasted_iota(jnp.int32, (256, 256), 1)
    regroup = (col == (row % 16) * 16 + row // 16).astype(jnp.bfloat16)
    branch_copy.wait()
    for s in range(count):
        br = [
            lax.dot_general(regroup, branch[r, s], NT, preferred_element_type=jnp.float32).astype(jnp.bfloat16)
            for r in range(2)
        ]
        lhs[s, 0:256, 0:256] = br[0]
        lhs[s, 0:256, 256:512] = -br[1]
        lhs[s, 256:512, 0:256] = br[1]
        lhs[s, 256:512, 256:512] = br[0]
    sends = []
    for w in range(4):
        copies[w].wait()
        for s in range(count):
            rhs = jnp.concatenate([stem[r, s, :, w].reshape(256, 256) for r in range(2)], axis=1)
            res = lax.dot_general(lhs[s], rhs, NT, preferred_element_type=jnp.float32).astype(jnp.bfloat16)
            for r in range(2):
                out[:, w, :, r, s] = res[r * 256 : (r + 1) * 256].reshape(8, 2, 16, 256)
        sends.append(pltpu.make_async_copy(out.at[:, w], out_hbm.at[:, w, :, :, part], out_sem.at[w]))
        sends[-1].start()
    for send in sends:
        send.wait()


def first_step(stem, branch, begin, count, filled=None):
    slices = stem.shape[1]
    operands = [stem, branch] + ([] if filled is None else [filled])
    return pl.pallas_call(
        functools.partial(first_kernel, begin, count),
        in_specs=[pl.BlockSpec(memory_space=pl.ANY)] * len(operands),
        out_specs=pl.BlockSpec(memory_space=pl.ANY),
        out_shape=jax.ShapeDtypeStruct((8, 4, 2, 2, slices, 16, 256), jnp.bfloat16),
        scratch_shapes=[
            pltpu.VMEM((2, count, 8, 4, 32, 256), jnp.bfloat16),
            pltpu.VMEM((2, count, 256, 256), jnp.bfloat16),
            pltpu.VMEM((count, 512, 512), jnp.bfloat16),
            pltpu.VMEM((8, 4, 2, 2, count, 16, 256), jnp.bfloat16),
            pltpu.SemaphoreType.DMA((4,)),
            pltpu.SemaphoreType.DMA,
            pltpu.SemaphoreType.DMA((4,)),
        ],
        input_output_aliases={} if filled is None else {2: 0},
        compiler_params=pltpu.CompilerParams(vmem_limit_bytes=56 << 20),
        cost_estimate=pl.CostEstimate(flops=12000000000, bytes_accessed=5 << 20, transcendentals=0),
        name="first_step",
    )(*operands)


def turn_kernel(me_ref, own_ref, other_ref, out_ref):
    first_core = me_ref[2] == 0
    for dx in range(RING):
        x = (me_ref[0] + dx) % RING
        for dy in range(RING):
            y = (me_ref[1] + dy) % RING
            at = pl.multiple_of((((x // 2) * RING + y) * 2 + x % 2) * 128, 128)
            for r in range(2):
                low = jnp.where(first_core, own_ref[dx, dy, r], other_ref[dx, dy, r])
                high = jnp.where(first_core, other_ref[dy, dx, r], own_ref[dy, dx, r])
                out_ref[r, :, pl.ds(at, 128)] = jnp.concatenate([low, high], axis=0).T


def turn_step(me, own, other):
    return pl.pallas_call(
        turn_kernel,
        in_specs=[pl.BlockSpec(memory_space=pltpu.SMEM)] + [pl.BlockSpec(memory_space=pltpu.VMEM)] * 2,
        out_specs=pl.BlockSpec(memory_space=pltpu.VMEM),
        out_shape=jax.ShapeDtypeStruct((2, 512, 2048), jnp.bfloat16),
        compiler_params=pltpu.CompilerParams(vmem_limit_bytes=32 << 20),
        cost_estimate=pl.CostEstimate(flops=18000000000, bytes_accessed=8 << 20, transcendentals=0),
        name="turn_step",
    )(me, own, other)


def second_kernel(x_hbm, b_hbm, out_hbm, x, b, held, out, x_sem, b_sem, out_sem):
    x_copies = [pltpu.make_async_copy(x_hbm.at[:, lh], x.at[lh], x_sem.at[lh]) for lh in range(2)]
    b_copies = [
        pltpu.make_async_copy(b_hbm.at[:, pl.ds(t * 128, 128)], b.at[:, pl.ds(t * 128, 128)], b_sem.at[t])
        for t in range(4)
    ]
    x_copies[0].start()
    b_copies[0].start()

    def dot(left, right):
        return lax.dot_general(left, right, NN, preferred_element_type=jnp.float32)

    sends = []
    for lh in range(2):
        x_copies[lh].wait()
        xr, xi = (x[lh, :, r].reshape(2048, 256) for r in range(2))
        for t in range(4):
            if lh == 0:
                b_copies[t].wait()
                if t == 0:
                    for copy in (*b_copies[1:], x_copies[1]):
                        copy.start()
            rows = slice(t * 128, (t + 1) * 128)
            br, bi = b[0, rows], b[1, rows]
            res = [dot(br, xr) + dot(-bi, xi), dot(bi, xr) + dot(br, xi)]
            res = [part.astype(jnp.bfloat16) for part in res]
            if lh == 0:
                for r in range(2):
                    held[r, rows] = res[r]
            else:
                parts = [held[0, rows], res[0], held[1, rows], res[1]]
                for za in range(8):
                    joined = jnp.concatenate([part[:, za * 32 : (za + 1) * 32] for part in parts], axis=1)
                    out[za, t * 2 : (t + 1) * 2] = joined.reshape(2, 64, 128)
                blocks = pl.ds(t * 2, 2)
                sends.append(pltpu.make_async_copy(out.at[:, blocks], out_hbm.at[:, blocks], out_sem.at[t]))
                sends[-1].start()
    for send in sends:
        send.wait()


def second_step(x, b2):
    shape = (8, 8, 64, 128)
    return pl.pallas_call(
        second_kernel,
        in_specs=[pl.BlockSpec(memory_space=pl.ANY)] * 2,
        out_specs=pl.BlockSpec(memory_space=pl.ANY),
        out_shape=jax.ShapeDtypeStruct(shape, jnp.bfloat16),
        scratch_shapes=[
            pltpu.VMEM((2, 32, 2, 64, 256), jnp.bfloat16),
            pltpu.VMEM((2, 512, 2048), jnp.bfloat16),
            pltpu.VMEM((2, 512, 256), jnp.bfloat16),
            pltpu.VMEM(shape, jnp.bfloat16),
            pltpu.SemaphoreType.DMA((2,)),
            pltpu.SemaphoreType.DMA((4,)),
            pltpu.SemaphoreType.DMA((4,)),
        ],
        compiler_params=pltpu.CompilerParams(vmem_limit_bytes=60 << 20),
        cost_estimate=pl.CostEstimate(flops=4300000000, bytes_accessed=9 << 20, transcendentals=0),
        name="second_step",
    )(x, b2)


def total_kernel(in_ref, out_ref):
    sums = []
    for i in range(8):
        acc = in_ref[0, i].astype(jnp.float32)
        for z in range(1, 8):
            acc = acc + in_ref[z, i].astype(jnp.float32)
        sums.append(acc)
    for r in range(2):
        out_ref[r, :, 0] = jnp.concatenate([acc[:, r * 64 : (r + 1) * 64] for acc in sums], axis=1)


def total_step(arrived):
    return pl.pallas_call(
        total_kernel,
        out_shape=jax.ShapeDtypeStruct((2, 64, 1, 512), jnp.float32),
        compiler_params=pltpu.CompilerParams(vmem_limit_bytes=16 << 20),
        cost_estimate=pl.CostEstimate(flops=1000000, bytes_accessed=2 << 20, transcendentals=0),
        name="total_step",
    )(arrived)


def place(x, y, core):
    return ((x // 2 * RING + y) * 2 + x % 2) * 2 + core


def ring_blocks(block, stage):
    blocks = [block]
    for d in range(1, RING):
        pairs = []
        for x in range(RING):
            for y in range(RING):
                for core in range(2):
                    along_y = core == stage
                    source = place(x, (y + d) % RING, core) if along_y else place((x + d) % RING, y, core)
                    pairs.append((source, place(x, y, core)))
        blocks.append(lax.ppermute(block, PLANE, pairs))
    return blocks


def pack_kernel(*refs):
    rows = refs[0].shape[0]
    for n, ref in enumerate(refs[:-1]):
        refs[-1][n * rows : (n + 1) * rows] = ref[...]


def pack(blocks):
    return pl.pallas_call(
        pack_kernel,
        in_specs=[pl.BlockSpec(memory_space=pltpu.VMEM)] * len(blocks),
        out_specs=pl.BlockSpec(memory_space=pltpu.VMEM),
        out_shape=jax.ShapeDtypeStruct((len(blocks) * blocks[0].shape[0], *blocks[0].shape[1:]), blocks[0].dtype),
        compiler_params=pltpu.CompilerParams(vmem_limit_bytes=24 << 20),
        cost_estimate=pl.CostEstimate(flops=1000000, bytes_accessed=1 << 20, transcendentals=0),
        name="pack",
    )(*blocks)


def shards(stem_tensor, branch_first, branch_second):
    slices = stem_tensor.shape[1]
    me = jnp.stack([lax.axis_index(ROWS), lax.axis_index("y"), lax.axis_index("core")]).astype(jnp.int32)
    stem = stem_tensor.reshape(2, slices, 8, 4, 32, 256)
    near = ring_blocks(branch_second.reshape(1, 2, slices * 16, 512), 0)
    sent = first_step(stem, branch_first, 0, slices).reshape(32, 2 * 2 * slices * 16, 256)
    sent, near = lax.optimization_barrier((sent, near))
    own = pack(ring_blocks(pack(near), 1))
    arrived = lax.all_to_all(sent, PLANE, split_axis=0, concat_axis=0, tiled=True)
    other = lax.ppermute(own, "core", [(0, 1), (1, 0)])
    grid = (RING, RING, 2, slices * 16, 512)
    turned = turn_step(me, own.reshape(grid), other.reshape(grid))
    partial = second_step(arrived.reshape(32, 2, 2, slices * 16, 256), turned)
    owned = lax.all_to_all(partial.reshape(64, 64, 128), OWNERS, split_axis=0, concat_axis=0, tiled=True)
    return total_step(owned.reshape(8, 8, 64, 128))


def solution(mesh):
    fine = Mesh(mesh.devices.reshape(2, 4, 8, 2, 2), ("xh", "y", "z", "xl", "core"))
    cuts, mode = ("xh", "y"), ("z", "xl", "core")
    in_specs = (
        P(None, cuts, mode, None, None, None),
        P(None, cuts, None, None),
        P(None, cuts, mode, None),
    )
    return jax.shard_map(
        shards, mesh=fine, in_specs=in_specs, out_specs=P(None, cuts, mode, None), check_vma=False
    )
```

```python
import functools

import jax
import jax.numpy as jnp
from jax import lax
from jax.experimental import pallas as pl
from jax.experimental.pallas import tpu as pltpu
from jax.sharding import Mesh
from jax.sharding import PartitionSpec as P

PLANE = ("xh", "y", "xl", "core")
CUTS = ("xh", "y")
MODE = ("z", "xl", "core")
ROWS = ("xh", "xl")
NT = (((1,), (1,)), ((), ()))
NN = (((1,), (0,)), ((), ()))
RING = 4
DEPTH = 8
ANY = pl.BlockSpec(memory_space=pl.ANY)
VMEM = pl.BlockSpec(memory_space=pltpu.VMEM)
SMEM = pl.BlockSpec(memory_space=pltpu.SMEM)


def first_kernel(lh, stem_hbm, branch_hbm, out_hbm, stem, branch, lhs, out, in_sem, branch_sem, out_sem):
    slices = stem.shape[1]
    stem_copies, branch_copies, sends = [], [], []
    for s in range(slices):
        branch_copies.append(pltpu.make_async_copy(branch_hbm.at[:, s], branch.at[:, s], branch_sem.at[s]))
        stem_copies.append(pltpu.make_async_copy(stem_hbm.at[:, s], stem.at[:, s], in_sem.at[s]))
        branch_copies[s].start()
        stem_copies[s].start()
    row = lax.broadcasted_iota(jnp.int32, (128, 256), 0)
    col = lax.broadcasted_iota(jnp.int32, (128, 256), 1)
    regroup = (col == (row % 16) * 16 + row // 16 * 2 + lh).astype(jnp.bfloat16)
    for s in range(slices):
        branch_copies[s].wait()
        br = [
            lax.dot_general(regroup, branch[r, s], NT, preferred_element_type=jnp.float32).astype(jnp.bfloat16)
            for r in range(2)
        ]
        lhs[s, 0:128, 0:256] = br[0]
        lhs[s, 0:128, 256:512] = -br[1]
        lhs[s, 128:256, 0:256] = br[1]
        lhs[s, 128:256, 256:512] = br[0]
        stem_copies[s].wait()
        for w in range(4):
            rhs = jnp.concatenate([stem[r, s, :, w].reshape(256, 256) for r in range(2)], axis=1)
            res = lax.dot_general(lhs[s], rhs, NT, preferred_element_type=jnp.float32).astype(jnp.bfloat16)
            for r in range(2):
                out[:, w, r, s] = res[r * 128 : (r + 1) * 128].reshape(8, 16, 256)
        sends.append(pltpu.make_async_copy(out.at[:, :, :, s], out_hbm.at[:, :, :, s], out_sem.at[s]))
        sends[s].start()
    for send in sends:
        send.wait()


def first_step(stem, branch, lh, flops):
    slices = stem.shape[1]
    shape = (8, 4, 2, slices, 16, 256)
    return pl.pallas_call(
        functools.partial(first_kernel, lh),
        in_specs=[ANY] * 2,
        out_specs=ANY,
        out_shape=jax.ShapeDtypeStruct(shape, jnp.bfloat16),
        scratch_shapes=[
            pltpu.VMEM(stem.shape, jnp.bfloat16),
            pltpu.VMEM(branch.shape, jnp.bfloat16),
            pltpu.VMEM((slices, 256, 512), jnp.bfloat16),
            pltpu.VMEM(shape, jnp.bfloat16),
            pltpu.SemaphoreType.DMA((slices,)),
            pltpu.SemaphoreType.DMA((slices,)),
            pltpu.SemaphoreType.DMA((slices,)),
        ],
        compiler_params=pltpu.CompilerParams(vmem_limit_bytes=56 << 20),
        cost_estimate=pl.CostEstimate(flops=flops, bytes_accessed=7 << 20, transcendentals=0),
        name="first_step",
    )(stem, branch)


def turn_kernel(me_ref, own_ref, other_ref, out_ref):
    first_core = me_ref[2] == 0
    for dx in range(RING):
        x = me_ref[0] ^ dx
        for dy in range(RING):
            y = me_ref[1] ^ dy
            at = pl.multiple_of((((x // 2) * RING + y) * 2 + x % 2) * 128, 128)
            for r in range(2):
                low = jnp.where(first_core, own_ref[dx, dy, r], other_ref[dx, dy, r])
                high = jnp.where(first_core, other_ref[dy, dx, r], own_ref[dy, dx, r])
                out_ref[r, :, pl.ds(at, 128)] = jnp.concatenate([low, high], axis=0).T


def turn_step(me, own, other):
    return pl.pallas_call(
        turn_kernel,
        in_specs=[SMEM, VMEM, VMEM],
        out_specs=VMEM,
        out_shape=jax.ShapeDtypeStruct((2, 512, 2048), jnp.bfloat16),
        compiler_params=pltpu.CompilerParams(vmem_limit_bytes=32 << 20),
        cost_estimate=pl.CostEstimate(flops=4000000000, bytes_accessed=8 << 20, transcendentals=0),
        name="turn_step",
    )(me, own, other)


def second_kernel(split, me_ref, x_hbm, b_hbm, *refs):
    x, b, out, x_sem, b_sem, out_sem = refs[-6:]
    out_hbm = refs[:-6]
    copies = [pltpu.make_async_copy(x_hbm, x, x_sem), pltpu.make_async_copy(b_hbm, b, b_sem)]
    for copy in copies:
        copy.start()

    def dot(left, right):
        return lax.dot_general(left, right, NN, preferred_element_type=jnp.float32)

    for copy in copies:
        copy.wait()
    xr, xi = (x[:, r].reshape(2048, 256) for r in range(2))
    for t in range(4):
        rows = slice(t * 128, (t + 1) * 128)
        br, bi = b[0, rows], b[1, rows]
        res = [dot(br, xr) + dot(-bi, xi), dot(bi, xr) + dot(br, xi)]
        res = [part.astype(jnp.bfloat16) for part in res]
        for q in range(2):
            parts = [res[r][q * 64 + jh * 32 : q * 64 + (jh + 1) * 32] for jh in range(2) for r in range(2)]
            for za in range(DEPTH):
                out[za, t * 2 + q] = jnp.concatenate([part[:, za * 32 : (za + 1) * 32] for part in parts], axis=1)
    sends = []
    for d in range(DEPTH):
        if split:
            sends.append(pltpu.make_async_copy(out.at[me_ref[3] ^ d], out_hbm[d], out_sem.at[d]))
        else:
            sends.append(pltpu.make_async_copy(out.at[d], out_hbm[0].at[d], out_sem.at[d]))
        sends[d].start()
    for send in sends:
        send.wait()


def second_step(me, x, b2, split):
    shape = (DEPTH, 8, 32, 128)
    if split:
        out_shape = [jax.ShapeDtypeStruct(shape[1:], jnp.bfloat16)] * DEPTH
    else:
        out_shape = [jax.ShapeDtypeStruct(shape, jnp.bfloat16)]
    return pl.pallas_call(
        functools.partial(second_kernel, split),
        in_specs=[SMEM, ANY, ANY],
        out_specs=[ANY] * len(out_shape),
        out_shape=out_shape,
        scratch_shapes=[
            pltpu.VMEM((32, 2, 64, 256), jnp.bfloat16),
            pltpu.VMEM((2, 512, 2048), jnp.bfloat16),
            pltpu.VMEM(shape, jnp.bfloat16),
            pltpu.SemaphoreType.DMA,
            pltpu.SemaphoreType.DMA,
            pltpu.SemaphoreType.DMA((DEPTH,)),
        ],
        compiler_params=pltpu.CompilerParams(vmem_limit_bytes=60 << 20),
        cost_estimate=pl.CostEstimate(flops=2150000000, bytes_accessed=7 << 20, transcendentals=0),
        name="second_step",
    )(me, x, b2)


def total_kernel(me_ref, *refs):
    blocks, outs, sums = refs[:DEPTH], refs[DEPTH:-1], refs[-1]
    acc = blocks[0][...].astype(jnp.float32)
    for block in blocks[1:]:
        acc = acc + block[...].astype(jnp.float32)
    sums[...] = acc
    for dy in range(RING):
        for dx in range(2):
            outs[dy][dx] = sums[(me_ref[0] // 2 ^ dx) * RING + (me_ref[1] ^ dy)]


def total_step(me, blocks):
    return pl.pallas_call(
        total_kernel,
        in_specs=[SMEM] + [VMEM] * DEPTH,
        out_specs=[VMEM] * RING,
        out_shape=[jax.ShapeDtypeStruct((2, 32, 128), jnp.float32)] * RING,
        scratch_shapes=[pltpu.VMEM((8, 32, 128), jnp.float32)],
        compiler_params=pltpu.CompilerParams(vmem_limit_bytes=16 << 20),
        cost_estimate=pl.CostEstimate(flops=10000000000, bytes_accessed=1 << 20, transcendentals=0),
        name="total_step",
    )(me, *blocks)


def pick_kernel(*refs):
    for n, ref in enumerate(refs[:-1]):
        refs[-1][n] = ref[1]


def pick_step(sums):
    return pl.pallas_call(
        pick_kernel,
        in_specs=[VMEM] * RING,
        out_specs=VMEM,
        out_shape=jax.ShapeDtypeStruct((RING, 32, 128), jnp.float32),
        compiler_params=pltpu.CompilerParams(vmem_limit_bytes=16 << 20),
        cost_estimate=pl.CostEstimate(flops=1000000, bytes_accessed=1 << 17, transcendentals=0),
        name="pick_step",
    )(*sums)


def lay_kernel(me_ref, later_ref, across_ref, *refs):
    out_ref, held = refs[-2:]
    xh = me_ref[0] // 2
    for dy in range(RING):
        held[xh * RING + (me_ref[1] ^ dy)] = refs[dy][0]
        held[(1 - xh) * RING + (me_ref[1] ^ dy)] = across_ref[dy]
    sums = []
    for i in range(8):
        acc = later_ref[0, i].astype(jnp.float32)
        for z in range(1, DEPTH):
            acc = acc + later_ref[z, i].astype(jnp.float32)
        sums.append((held[i], acc))
    for r in range(2):
        for jh in range(2):
            at = jh * 64 + r * 32
            out_ref[r, jh * 32 : (jh + 1) * 32, 0] = jnp.concatenate(
                [half[:, at : at + 32] for pair in sums for half in pair], axis=1
            )


def lay_step(me, later, across, sums):
    return pl.pallas_call(
        lay_kernel,
        in_specs=[SMEM] + [VMEM] * (2 + RING),
        out_specs=VMEM,
        out_shape=jax.ShapeDtypeStruct((2, 64, 1, 512), jnp.float32),
        scratch_shapes=[pltpu.VMEM((8, 32, 128), jnp.float32)],
        compiler_params=pltpu.CompilerParams(vmem_limit_bytes=16 << 20),
        cost_estimate=pl.CostEstimate(flops=1000000, bytes_accessed=1 << 20, transcendentals=0),
        name="lay_step",
    )(me, later, across, *sums)


def place(x, y, core):
    return ((x // 2 * RING + y) * 2 + x % 2) * 2 + core


def ring_blocks(block, stage):
    blocks = [block]
    for d in range(1, RING):
        pairs = []
        for x in range(RING):
            for y in range(RING):
                for core in range(2):
                    along_y = core == stage
                    source = place(x, y ^ d, core) if along_y else place(x ^ d, y, core)
                    pairs.append((source, place(x, y, core)))
        blocks.append(lax.ppermute(block, PLANE, pairs))
    return blocks


def pack_kernel(*refs):
    rows = refs[0].shape[0]
    for n, ref in enumerate(refs[:-1]):
        refs[-1][n * rows : (n + 1) * rows] = ref[...]


def pack(blocks):
    return pl.pallas_call(
        pack_kernel,
        in_specs=[VMEM] * len(blocks),
        out_specs=VMEM,
        out_shape=jax.ShapeDtypeStruct((len(blocks) * blocks[0].shape[0], *blocks[0].shape[1:]), blocks[0].dtype),
        compiler_params=pltpu.CompilerParams(vmem_limit_bytes=24 << 20),
        cost_estimate=pl.CostEstimate(flops=1000000, bytes_accessed=1 << 20, transcendentals=0),
        name="pack",
    )(*blocks)


def exchange(block, axes):
    return lax.all_to_all(block, axes, split_axis=0, concat_axis=0, tiled=True)


def shards(stem_tensor, branch_first, branch_second):
    slices = stem_tensor.shape[1]
    me = [lax.axis_index(axis) for axis in (ROWS, "y", "core", "z")]
    me = jnp.stack(me).astype(jnp.int32)
    stem = stem_tensor.reshape(2, slices, 8, 4, 32, 256)
    near = ring_blocks(branch_second.reshape(1, 2, slices * 16, 512), 0)
    sent = first_step(stem, branch_first, 0, 1200000000)
    sent, near, stem = lax.optimization_barrier((sent, near, stem))
    own = pack(ring_blocks(pack(near), 1))
    arrived = exchange(sent.reshape(32, 2 * slices * 16, 256), PLANE)
    later = first_step(stem, branch_first, 1, 20000000000)
    arrived, later = lax.optimization_barrier((arrived, later))
    other = lax.ppermute(own, "core", [(0, 1), (1, 0)])
    blocks = (RING, RING, 2, slices * 16, 512)
    turned = turn_step(me, own.reshape(blocks), other.reshape(blocks))
    later = exchange(later.reshape(32, 2 * slices * 16, 256), PLANE)
    half = list(second_step(me, arrived.reshape(32, 2, slices * 16, 256), turned, True))
    for d in range(1, DEPTH):
        half[d] = lax.ppermute(half[d], "z", [(z, z ^ d) for z in range(DEPTH)])
    early = (0, 1, 2, 3)
    later, *done = lax.optimization_barrier((later, *[half[d] for d in early]))
    for d, block in zip(early, done):
        half[d] = block
    (rest,) = second_step(me, later.reshape(32, 2, slices * 16, 256), turned, False)
    rest = exchange(rest.reshape(64, 32, 128), ("z",) + CUTS)
    sums = list(total_step(me, half))
    for dy in range(1, RING):
        sums[dy] = lax.ppermute(sums[dy], "y", [(y, y ^ dy) for y in range(RING)])
    across = lax.ppermute(pick_step(sums), "xh", [(0, 1), (1, 0)])
    return lay_step(me, rest.reshape(DEPTH, 8, 32, 128), across, sums)


def solution(mesh):
    fine = Mesh(mesh.devices.reshape(2, RING, DEPTH, 2, 2), ("xh", "y", "z", "xl", "core"))
    in_specs = (
        P(None, CUTS, MODE, None, None, None),
        P(None, CUTS, None, None),
        P(None, CUTS, MODE, None),
    )
    return jax.shard_map(
        shards, mesh=fine, in_specs=in_specs, out_specs=P(None, CUTS, MODE, None), check_vma=False
    )
```

```python
import functools

import jax
import jax.numpy as jnp
from jax import lax
from jax.experimental import pallas as pl
from jax.experimental.pallas import tpu as pltpu
from jax.sharding import Mesh
from jax.sharding import PartitionSpec as P

PLANE = ("xh", "y", "xl", "core")
CUTS = ("xh", "y")
MODE = ("z", "xl", "core")
ROWS = ("xh", "xl")
NT = (((1,), (1,)), ((), ()))
NN = (((1,), (0,)), ((), ()))
RING = 4
DEPTH = 8
ANY = pl.BlockSpec(memory_space=pl.ANY)
VMEM = pl.BlockSpec(memory_space=pltpu.VMEM)
SMEM = pl.BlockSpec(memory_space=pltpu.SMEM)


def first_kernel(lh, stem_hbm, branch_hbm, out_hbm, stem, branch, lhs, out, in_sem, branch_sem, out_sem):
    slices = stem.shape[1]
    stem_copies, branch_copies, sends = [], [], []
    for s in range(slices):
        branch_copies.append(pltpu.make_async_copy(branch_hbm.at[:, s], branch.at[:, s], branch_sem.at[s]))
        stem_copies.append(pltpu.make_async_copy(stem_hbm.at[:, s], stem.at[:, s], in_sem.at[s]))
        branch_copies[s].start()
        stem_copies[s].start()
    row = lax.broadcasted_iota(jnp.int32, (128, 256), 0)
    col = lax.broadcasted_iota(jnp.int32, (128, 256), 1)
    regroup = (col == (row % 16) * 16 + row // 16 * 2 + lh).astype(jnp.bfloat16)
    for s in range(slices):
        branch_copies[s].wait()
        br = [
            lax.dot_general(regroup, branch[r, s], NT, preferred_element_type=jnp.float32).astype(jnp.bfloat16)
            for r in range(2)
        ]
        lhs[s, 0:128, 0:256] = br[0]
        lhs[s, 0:128, 256:512] = -br[1]
        lhs[s, 128:256, 0:256] = br[1]
        lhs[s, 128:256, 256:512] = br[0]
        stem_copies[s].wait()
        for w in range(4):
            rhs = jnp.concatenate([stem[r, s, :, w].reshape(256, 256) for r in range(2)], axis=1)
            res = lax.dot_general(lhs[s], rhs, NT, preferred_element_type=jnp.float32).astype(jnp.bfloat16)
            for r in range(2):
                out[:, w, r, s] = res[r * 128 : (r + 1) * 128].reshape(8, 16, 256)
        sends.append(pltpu.make_async_copy(out.at[:, :, :, s], out_hbm.at[:, :, :, s], out_sem.at[s]))
        sends[s].start()
    for send in sends:
        send.wait()


def first_step(stem, branch, lh, flops):
    slices = stem.shape[1]
    shape = (8, 4, 2, slices, 16, 256)
    return pl.pallas_call(
        functools.partial(first_kernel, lh),
        in_specs=[ANY] * 2,
        out_specs=ANY,
        out_shape=jax.ShapeDtypeStruct(shape, jnp.bfloat16),
        scratch_shapes=[
            pltpu.VMEM(stem.shape, jnp.bfloat16),
            pltpu.VMEM(branch.shape, jnp.bfloat16),
            pltpu.VMEM((slices, 256, 512), jnp.bfloat16),
            pltpu.VMEM(shape, jnp.bfloat16),
            pltpu.SemaphoreType.DMA((slices,)),
            pltpu.SemaphoreType.DMA((slices,)),
            pltpu.SemaphoreType.DMA((slices,)),
        ],
        compiler_params=pltpu.CompilerParams(vmem_limit_bytes=56 << 20),
        cost_estimate=pl.CostEstimate(flops=flops, bytes_accessed=7 << 20, transcendentals=0),
        name="first_step",
    )(stem, branch)


def turn_kernel(me_ref, *refs):
    own, other, (out_hbm, out, out_sem) = refs[:RING], refs[RING : 2 * RING], refs[2 * RING :]
    first_core = me_ref[2] == 0
    sends = []
    for r in range(2):
        for dx in range(RING):
            x = me_ref[0] ^ dx
            for dy in range(RING):
                y = me_ref[1] ^ dy
                at = pl.multiple_of((((x // 2) * RING + y) * 2 + x % 2) * 128, 128)
                low = jnp.where(first_core, own[dx][dy, r], other[dx][dy, r])
                high = jnp.where(first_core, other[dy][dx, r], own[dy][dx, r])
                out[r, :, pl.ds(at, 128)] = jnp.concatenate([low, high], axis=0).T
        sends.append(pltpu.make_async_copy(out.at[r], out_hbm.at[r], out_sem.at[r]))
        sends[r].start()
    for send in sends:
        send.wait()


def turn_step(me, own, other):
    return pl.pallas_call(
        turn_kernel,
        in_specs=[SMEM] + [VMEM] * (2 * RING),
        out_specs=ANY,
        out_shape=jax.ShapeDtypeStruct((2, 512, 2048), jnp.bfloat16),
        scratch_shapes=[pltpu.VMEM((2, 512, 2048), jnp.bfloat16), pltpu.SemaphoreType.DMA((2,))],
        compiler_params=pltpu.CompilerParams(vmem_limit_bytes=56 << 20),
        cost_estimate=pl.CostEstimate(flops=10000000000, bytes_accessed=8 << 20, transcendentals=0),
        name="turn_step",
    )(me, *own, *other)


def second_kernel(split, me_ref, x_hbm, b_hbm, *refs):
    x, b, out, x_sem, b_sem, out_sem = refs[-6:]
    out_hbm = refs[:-6]
    x_copy = pltpu.make_async_copy(x_hbm, x, x_sem)
    b_copies = [
        pltpu.make_async_copy(b_hbm.at[:, pl.ds(h * 256, 256)], b.at[:, pl.ds(h * 256, 256)], b_sem.at[h])
        for h in range(2)
    ]
    for copy in (x_copy, *b_copies):
        copy.start()

    def dot(left, right):
        return lax.dot_general(left, right, NN, preferred_element_type=jnp.float32)

    x_copy.wait()
    xr, xi = (x[:, r].reshape(2048, 256) for r in range(2))
    sends = []
    for t in range(4):
        if t % 2 == 0:
            b_copies[t // 2].wait()
        rows = slice(t * 128, (t + 1) * 128)
        br, bi = b[0, rows], b[1, rows]
        res = [dot(br, xr) + dot(-bi, xi), dot(bi, xr) + dot(br, xi)]
        res = [part.astype(jnp.bfloat16) for part in res]
        for q in range(2):
            parts = [res[r][q * 64 + jh * 32 : q * 64 + (jh + 1) * 32] for jh in range(2) for r in range(2)]
            for za in range(DEPTH):
                out[za, t * 2 + q] = jnp.concatenate([part[:, za * 32 : (za + 1) * 32] for part in parts], axis=1)
        if t % 2 == 1 and not split:
            part = pl.ds(t * 2 - 2, 4)
            sends.append(pltpu.make_async_copy(out.at[:, part], out_hbm[0].at[:, part], out_sem.at[t // 2]))
            sends[-1].start()
    if split:
        for d in range(DEPTH):
            sends.append(pltpu.make_async_copy(out.at[me_ref[3] ^ d], out_hbm[d], out_sem.at[d]))
            sends[-1].start()
    for send in sends:
        send.wait()


def second_step(me, x, b2, split):
    shape = (DEPTH, 8, 32, 128)
    if split:
        out_shape = [jax.ShapeDtypeStruct(shape[1:], jnp.bfloat16)] * DEPTH
    else:
        out_shape = [jax.ShapeDtypeStruct(shape, jnp.bfloat16)]
    return pl.pallas_call(
        functools.partial(second_kernel, split),
        in_specs=[SMEM, ANY, ANY],
        out_specs=[ANY] * len(out_shape),
        out_shape=out_shape,
        scratch_shapes=[
            pltpu.VMEM((32, 2, 64, 256), jnp.bfloat16),
            pltpu.VMEM((2, 512, 2048), jnp.bfloat16),
            pltpu.VMEM(shape, jnp.bfloat16),
            pltpu.SemaphoreType.DMA,
            pltpu.SemaphoreType.DMA((2,)),
            pltpu.SemaphoreType.DMA((DEPTH,)),
        ],
        compiler_params=pltpu.CompilerParams(vmem_limit_bytes=(24 if split else 60) << 20),
        cost_estimate=pl.CostEstimate(flops=2150000000, bytes_accessed=7 << 20, transcendentals=0),
        name="second_step",
    )(me, x, b2)


def total_kernel(me_ref, *refs):
    blocks, outs, sums = refs[:DEPTH], refs[DEPTH:-1], refs[-1]
    acc = blocks[0][...].astype(jnp.float32)
    for block in blocks[1:]:
        acc = acc + block[...].astype(jnp.float32)
    sums[...] = acc
    for dy in range(RING):
        for dx in range(2):
            outs[dy][dx] = sums[(me_ref[0] // 2 ^ dx) * RING + (me_ref[1] ^ dy)]


def total_step(me, blocks):
    return pl.pallas_call(
        total_kernel,
        in_specs=[SMEM] + [VMEM] * DEPTH,
        out_specs=[VMEM] * RING,
        out_shape=[jax.ShapeDtypeStruct((2, 32, 128), jnp.float32)] * RING,
        scratch_shapes=[pltpu.VMEM((8, 32, 128), jnp.float32)],
        compiler_params=pltpu.CompilerParams(vmem_limit_bytes=16 << 20),
        cost_estimate=pl.CostEstimate(flops=10000000000, bytes_accessed=1 << 20, transcendentals=0),
        name="total_step",
    )(me, *blocks)


def pick_kernel(*refs):
    for n, ref in enumerate(refs[:-1]):
        refs[-1][n] = ref[1]


def pick_step(sums):
    return pl.pallas_call(
        pick_kernel,
        in_specs=[VMEM] * RING,
        out_specs=VMEM,
        out_shape=jax.ShapeDtypeStruct((RING, 32, 128), jnp.float32),
        compiler_params=pltpu.CompilerParams(vmem_limit_bytes=16 << 20),
        cost_estimate=pl.CostEstimate(flops=1000000, bytes_accessed=1 << 17, transcendentals=0),
        name="pick_step",
    )(*sums)


def lay_kernel(me_ref, later_ref, across_ref, *refs):
    out_ref, held = refs[-2:]
    xh = me_ref[0] // 2
    for dy in range(RING):
        held[xh * RING + (me_ref[1] ^ dy)] = refs[dy][0]
        held[(1 - xh) * RING + (me_ref[1] ^ dy)] = across_ref[dy]
    sums = []
    for i in range(8):
        acc = later_ref[0, i].astype(jnp.float32)
        for z in range(1, DEPTH):
            acc = acc + later_ref[z, i].astype(jnp.float32)
        sums.append((held[i], acc))
    for r in range(2):
        for jh in range(2):
            at = jh * 64 + r * 32
            out_ref[r, jh * 32 : (jh + 1) * 32, 0] = jnp.concatenate(
                [half[:, at : at + 32] for pair in sums for half in pair], axis=1
            )


def lay_step(me, later, across, sums):
    return pl.pallas_call(
        lay_kernel,
        in_specs=[SMEM] + [VMEM] * (2 + RING),
        out_specs=VMEM,
        out_shape=jax.ShapeDtypeStruct((2, 64, 1, 512), jnp.float32),
        scratch_shapes=[pltpu.VMEM((8, 32, 128), jnp.float32)],
        compiler_params=pltpu.CompilerParams(vmem_limit_bytes=16 << 20),
        cost_estimate=pl.CostEstimate(flops=1000000, bytes_accessed=1 << 20, transcendentals=0),
        name="lay_step",
    )(me, later, across, *sums)


def place(x, y, core):
    return ((x // 2 * RING + y) * 2 + x % 2) * 2 + core


def ring_blocks(block, stage):
    blocks = [block]
    for d in range(1, RING):
        pairs = []
        for x in range(RING):
            for y in range(RING):
                for core in range(2):
                    along_y = core == stage
                    source = place(x, y ^ d, core) if along_y else place(x ^ d, y, core)
                    pairs.append((source, place(x, y, core)))
        blocks.append(lax.ppermute(block, PLANE, pairs))
    return blocks


def pack_kernel(*refs):
    rows = refs[0].shape[0]
    for n, ref in enumerate(refs[:-1]):
        refs[-1][n * rows : (n + 1) * rows] = ref[...]


def pack(blocks):
    return pl.pallas_call(
        pack_kernel,
        in_specs=[VMEM] * len(blocks),
        out_specs=VMEM,
        out_shape=jax.ShapeDtypeStruct((len(blocks) * blocks[0].shape[0], *blocks[0].shape[1:]), blocks[0].dtype),
        compiler_params=pltpu.CompilerParams(vmem_limit_bytes=24 << 20),
        cost_estimate=pl.CostEstimate(flops=1000000, bytes_accessed=1 << 20, transcendentals=0),
        name="pack",
    )(*blocks)


def exchange(block, axes):
    return lax.all_to_all(block, axes, split_axis=0, concat_axis=0, tiled=True)


def shards(stem_tensor, branch_first, branch_second):
    slices = stem_tensor.shape[1]
    me = [lax.axis_index(axis) for axis in (ROWS, "y", "core", "z")]
    me = jnp.stack(me).astype(jnp.int32)
    stem = stem_tensor.reshape(2, slices, 8, 4, 32, 256)
    near = ring_blocks(branch_second.reshape(1, 2, slices * 16, 512), 0)
    sent = first_step(stem, branch_first, 0, 1200000000)
    sent, near, stem = lax.optimization_barrier((sent, near, stem))
    own = ring_blocks(pack(near), 1)
    arrived = exchange(sent.reshape(32, 2 * slices * 16, 256), PLANE)
    later = first_step(stem, branch_first, 1, 10000000000)
    other = [lax.ppermute(block, "core", [(0, 1), (1, 0)]) for block in own]
    blocks = (RING, 2, slices * 16, 512)
    own, other = ([block.reshape(blocks) for block in part] for part in (own, other))
    turned = turn_step(me, own, other)
    arrived, later, turned = lax.optimization_barrier((arrived, later, turned))
    later = exchange(later.reshape(32, 2 * slices * 16, 256), PLANE)
    half = list(second_step(me, arrived.reshape(32, 2, slices * 16, 256), turned, True))
    for d in range(1, DEPTH):
        half[d] = lax.ppermute(half[d], "z", [(z, z ^ d) for z in range(DEPTH)])
    early = (0, 1, 2, 3)
    later, *done = lax.optimization_barrier((later, *[half[d] for d in early]))
    for d, block in zip(early, done):
        half[d] = block
    (rest,) = second_step(me, later.reshape(32, 2, slices * 16, 256), turned, False)
    rest = exchange(rest.reshape(64, 32, 128), ("z",) + CUTS)
    sums = list(total_step(me, half))
    for dy in range(1, RING):
        sums[dy] = lax.ppermute(sums[dy], "y", [(y, y ^ dy) for y in range(RING)])
    across = lax.ppermute(pick_step(sums), "xh", [(0, 1), (1, 0)])
    return lay_step(me, rest.reshape(DEPTH, 8, 32, 128), across, sums)


def solution(mesh):
    fine = Mesh(mesh.devices.reshape(2, RING, DEPTH, 2, 2), ("xh", "y", "z", "xl", "core"))
    in_specs = (
        P(None, CUTS, MODE, None, None, None),
        P(None, CUTS, None, None),
        P(None, CUTS, MODE, None),
    )
    return jax.shard_map(
        shards, mesh=fine, in_specs=in_specs, out_specs=P(None, CUTS, MODE, None), check_vma=False
    )
```

```python
import functools

import jax
import jax.numpy as jnp
from jax import lax
from jax.experimental import pallas as pl
from jax.experimental.pallas import tpu as pltpu
from jax.sharding import Mesh
from jax.sharding import PartitionSpec as P

PLANE = ("xh", "y", "xl", "core")
CUTS = ("xh", "y")
MODE = ("z", "xl", "core")
ROWS = ("xh", "xl")
NT = (((1,), (1,)), ((), ()))
NN = (((1,), (0,)), ((), ()))
RING = 4
DEPTH = 8
ANY = pl.BlockSpec(memory_space=pl.ANY)
VMEM = pl.BlockSpec(memory_space=pltpu.VMEM)
SMEM = pl.BlockSpec(memory_space=pltpu.SMEM)


def first_kernel(lh, stem_hbm, branch_hbm, out_hbm, stem, branch, lhs, out, in_sem, branch_sem, out_sem):
    slices = stem.shape[1]
    stem_copies, branch_copies, sends = [], [], []
    for s in range(slices):
        branch_copies.append(pltpu.make_async_copy(branch_hbm.at[:, s], branch.at[:, s], branch_sem.at[s]))
        stem_copies.append(pltpu.make_async_copy(stem_hbm.at[:, s], stem.at[:, s], in_sem.at[s]))
        branch_copies[s].start()
        stem_copies[s].start()
    row = lax.broadcasted_iota(jnp.int32, (128, 256), 0)
    col = lax.broadcasted_iota(jnp.int32, (128, 256), 1)
    regroup = (col == (row % 16) * 16 + row // 16 * 2 + lh).astype(jnp.bfloat16)
    for s in range(slices):
        branch_copies[s].wait()
        br = [
            lax.dot_general(regroup, branch[r, s], NT, preferred_element_type=jnp.float32).astype(jnp.bfloat16)
            for r in range(2)
        ]
        lhs[s, 0:128, 0:256] = br[0]
        lhs[s, 0:128, 256:512] = -br[1]
        lhs[s, 128:256, 0:256] = br[1]
        lhs[s, 128:256, 256:512] = br[0]
        stem_copies[s].wait()
        for w in range(4):
            rhs = jnp.concatenate([stem[r, s, :, w].reshape(256, 256) for r in range(2)], axis=1)
            res = lax.dot_general(lhs[s], rhs, NT, preferred_element_type=jnp.float32).astype(jnp.bfloat16)
            for r in range(2):
                out[:, w, r, s] = res[r * 128 : (r + 1) * 128].reshape(8, 16, 256)
        sends.append(pltpu.make_async_copy(out.at[:, :, :, s], out_hbm.at[:, :, :, s], out_sem.at[s]))
        sends[s].start()
    for send in sends:
        send.wait()


def first_step(stem, branch, lh, flops):
    slices = stem.shape[1]
    shape = (8, 4, 2, slices, 16, 256)
    return pl.pallas_call(
        functools.partial(first_kernel, lh),
        in_specs=[ANY] * 2,
        out_specs=ANY,
        out_shape=jax.ShapeDtypeStruct(shape, jnp.bfloat16),
        scratch_shapes=[
            pltpu.VMEM(stem.shape, jnp.bfloat16),
            pltpu.VMEM(branch.shape, jnp.bfloat16),
            pltpu.VMEM((slices, 256, 512), jnp.bfloat16),
            pltpu.VMEM(shape, jnp.bfloat16),
            pltpu.SemaphoreType.DMA((slices,)),
            pltpu.SemaphoreType.DMA((slices,)),
            pltpu.SemaphoreType.DMA((slices,)),
        ],
        compiler_params=pltpu.CompilerParams(vmem_limit_bytes=56 << 20),
        cost_estimate=pl.CostEstimate(flops=flops, bytes_accessed=7 << 20, transcendentals=0),
        name="first_step",
    )(stem, branch)


def turn_kernel(me_ref, *refs):
    own, other, out_ref = refs[:RING], refs[RING:-1], refs[-1]
    first_core = me_ref[2] == 0
    for dx in range(RING):
        x = me_ref[0] ^ dx
        for dy in range(RING):
            y = me_ref[1] ^ dy
            at = pl.multiple_of((((x // 2) * RING + y) * 2 + x % 2) * 128, 128)
            for r in range(2):
                low = jnp.where(first_core, own[dx][dy, r], other[dx][dy, r])
                high = jnp.where(first_core, other[dy][dx, r], own[dy][dx, r])
                out_ref[r, :, pl.ds(at, 128)] = jnp.concatenate([low, high], axis=0).T


def turn_step(me, own, other):
    return pl.pallas_call(
        turn_kernel,
        in_specs=[SMEM] + [VMEM] * (2 * RING),
        out_specs=VMEM,
        out_shape=jax.ShapeDtypeStruct((2, 512, 2048), jnp.bfloat16),
        compiler_params=pltpu.CompilerParams(vmem_limit_bytes=24 << 20),
        cost_estimate=pl.CostEstimate(flops=10000000000, bytes_accessed=8 << 20, transcendentals=0),
        name="turn_step",
    )(me, *own, *other)


def second_kernel(split, me_ref, x_hbm, b_hbm, *refs):
    x, b, out, x_sem, b_sem, out_sem = refs[-6:]
    out_hbm = refs[:-6]
    x_copy = pltpu.make_async_copy(x_hbm, x, x_sem)
    b_copies = [
        pltpu.make_async_copy(b_hbm.at[:, pl.ds(h * 256, 256)], b.at[:, pl.ds(h * 256, 256)], b_sem.at[h])
        for h in range(2)
    ]
    for copy in (x_copy, *b_copies):
        copy.start()

    def dot(left, right):
        return lax.dot_general(left, right, NN, preferred_element_type=jnp.float32)

    x_copy.wait()
    xr, xi = (x[:, r].reshape(2048, 256) for r in range(2))
    sends = []
    for t in range(4):
        if t % 2 == 0:
            b_copies[t // 2].wait()
        rows = slice(t * 128, (t + 1) * 128)
        br, bi = b[0, rows], b[1, rows]
        res = [dot(br, xr) + dot(-bi, xi), dot(bi, xr) + dot(br, xi)]
        res = [part.astype(jnp.bfloat16) for part in res]
        for q in range(2):
            parts = [res[r][q * 64 + jh * 32 : q * 64 + (jh + 1) * 32] for jh in range(2) for r in range(2)]
            for za in range(DEPTH):
                out[za, t * 2 + q] = jnp.concatenate([part[:, za * 32 : (za + 1) * 32] for part in parts], axis=1)
        if t % 2 == 1 and not split:
            part = pl.ds(t * 2 - 2, 4)
            sends.append(pltpu.make_async_copy(out.at[:, part], out_hbm[0].at[:, part], out_sem.at[t // 2]))
            sends[-1].start()
    if split:
        for d in range(DEPTH):
            sends.append(pltpu.make_async_copy(out.at[me_ref[3] ^ d], out_hbm[d], out_sem.at[d]))
            sends[-1].start()
    for send in sends:
        send.wait()


def second_step(me, x, b2, split):
    shape = (DEPTH, 8, 32, 128)
    if split:
        out_shape = [jax.ShapeDtypeStruct(shape[1:], jnp.bfloat16)] * DEPTH
    else:
        out_shape = [jax.ShapeDtypeStruct(shape, jnp.bfloat16)]
    return pl.pallas_call(
        functools.partial(second_kernel, split),
        in_specs=[SMEM, ANY, ANY],
        out_specs=[ANY] * len(out_shape),
        out_shape=out_shape,
        scratch_shapes=[
            pltpu.VMEM((32, 2, 64, 256), jnp.bfloat16),
            pltpu.VMEM((2, 512, 2048), jnp.bfloat16),
            pltpu.VMEM(shape, jnp.bfloat16),
            pltpu.SemaphoreType.DMA,
            pltpu.SemaphoreType.DMA((2,)),
            pltpu.SemaphoreType.DMA((DEPTH,)),
        ],
        compiler_params=pltpu.CompilerParams(vmem_limit_bytes=(24 if split else 60) << 20),
        cost_estimate=pl.CostEstimate(flops=2150000000, bytes_accessed=7 << 20, transcendentals=0),
        name="second_step",
    )(me, x, b2)


def total_kernel(me_ref, *refs):
    blocks, outs, sums = refs[:DEPTH], refs[DEPTH:-1], refs[-1]
    acc = blocks[0][...].astype(jnp.float32)
    for block in blocks[1:]:
        acc = acc + block[...].astype(jnp.float32)
    sums[...] = acc
    for dy in range(RING):
        for dx in range(2):
            outs[dy][dx] = sums[(me_ref[0] // 2 ^ dx) * RING + (me_ref[1] ^ dy)]


def total_step(me, blocks):
    return pl.pallas_call(
        total_kernel,
        in_specs=[SMEM] + [VMEM] * DEPTH,
        out_specs=[VMEM] * RING,
        out_shape=[jax.ShapeDtypeStruct((2, 32, 128), jnp.float32)] * RING,
        scratch_shapes=[pltpu.VMEM((8, 32, 128), jnp.float32)],
        compiler_params=pltpu.CompilerParams(vmem_limit_bytes=16 << 20),
        cost_estimate=pl.CostEstimate(flops=10000000000, bytes_accessed=1 << 20, transcendentals=0),
        name="total_step",
    )(me, *blocks)


def pick_kernel(*refs):
    for n, ref in enumerate(refs[:-1]):
        refs[-1][n] = ref[1]


def pick_step(sums):
    return pl.pallas_call(
        pick_kernel,
        in_specs=[VMEM] * RING,
        out_specs=VMEM,
        out_shape=jax.ShapeDtypeStruct((RING, 32, 128), jnp.float32),
        compiler_params=pltpu.CompilerParams(vmem_limit_bytes=16 << 20),
        cost_estimate=pl.CostEstimate(flops=1000000, bytes_accessed=1 << 17, transcendentals=0),
        name="pick_step",
    )(*sums)


def lay_kernel(me_ref, later_ref, across_ref, *refs):
    out_ref, held = refs[-2:]
    xh = me_ref[0] // 2
    for dy in range(RING):
        held[xh * RING + (me_ref[1] ^ dy)] = refs[dy][0]
        held[(1 - xh) * RING + (me_ref[1] ^ dy)] = across_ref[dy]
    sums = []
    for i in range(8):
        acc = later_ref[0, i].astype(jnp.float32)
        for z in range(1, DEPTH):
            acc = acc + later_ref[z, i].astype(jnp.float32)
        sums.append((held[i], acc))
    for r in range(2):
        for jh in range(2):
            at = jh * 64 + r * 32
            out_ref[r, jh * 32 : (jh + 1) * 32, 0] = jnp.concatenate(
                [half[:, at : at + 32] for pair in sums for half in pair], axis=1
            )


def lay_step(me, later, across, sums):
    return pl.pallas_call(
        lay_kernel,
        in_specs=[SMEM] + [VMEM] * (2 + RING),
        out_specs=VMEM,
        out_shape=jax.ShapeDtypeStruct((2, 64, 1, 512), jnp.float32),
        scratch_shapes=[pltpu.VMEM((8, 32, 128), jnp.float32)],
        compiler_params=pltpu.CompilerParams(vmem_limit_bytes=16 << 20),
        cost_estimate=pl.CostEstimate(flops=1000000, bytes_accessed=1 << 20, transcendentals=0),
        name="lay_step",
    )(me, later, across, *sums)


def place(x, y, core):
    return ((x // 2 * RING + y) * 2 + x % 2) * 2 + core


def ring_blocks(block, stage):
    blocks = [block]
    for d in range(1, RING):
        pairs = []
        for x in range(RING):
            for y in range(RING):
                for core in range(2):
                    along_y = core == stage
                    source = place(x, y ^ d, core) if along_y else place(x ^ d, y, core)
                    pairs.append((source, place(x, y, core)))
        blocks.append(lax.ppermute(block, PLANE, pairs))
    return blocks


def pack_kernel(*refs):
    rows = refs[0].shape[0]
    for n, ref in enumerate(refs[:-1]):
        refs[-1][n * rows : (n + 1) * rows] = ref[...]


def pack(blocks):
    return pl.pallas_call(
        pack_kernel,
        in_specs=[VMEM] * len(blocks),
        out_specs=VMEM,
        out_shape=jax.ShapeDtypeStruct((len(blocks) * blocks[0].shape[0], *blocks[0].shape[1:]), blocks[0].dtype),
        compiler_params=pltpu.CompilerParams(vmem_limit_bytes=24 << 20),
        cost_estimate=pl.CostEstimate(flops=1000000, bytes_accessed=1 << 20, transcendentals=0),
        name="pack",
    )(*blocks)


def exchange(block, axes):
    return lax.all_to_all(block, axes, split_axis=0, concat_axis=0, tiled=True)


def shards(stem_tensor, branch_first, branch_second):
    slices = stem_tensor.shape[1]
    me = [lax.axis_index(axis) for axis in (ROWS, "y", "core", "z")]
    me = jnp.stack(me).astype(jnp.int32)
    stem = stem_tensor.reshape(2, slices, 8, 4, 32, 256)
    near = ring_blocks(branch_second.reshape(1, 2, slices * 16, 512), 0)
    sent = first_step(stem, branch_first, 0, 1200000000)
    sent, near, stem = lax.optimization_barrier((sent, near, stem))
    own = ring_blocks(pack(near), 1)
    arrived = exchange(sent.reshape(32, 2 * slices * 16, 256), PLANE)
    later = first_step(stem, branch_first, 1, 1000000)
    other = [lax.ppermute(block, "core", [(0, 1), (1, 0)]) for block in own]
    blocks = (RING, 2, slices * 16, 512)
    own, other = ([block.reshape(blocks) for block in part] for part in (own, other))
    turned = turn_step(me, own, other)
    arrived, later = lax.optimization_barrier((arrived, later))
    later = exchange(later.reshape(32, 2 * slices * 16, 256), PLANE)
    half = list(second_step(me, arrived.reshape(32, 2, slices * 16, 256), turned, True))
    for d in range(1, DEPTH):
        half[d] = lax.ppermute(half[d], "z", [(z, z ^ d) for z in range(DEPTH)])
    early = (0, 1, 2, 3)
    later, *done = lax.optimization_barrier((later, *[half[d] for d in early]))
    for d, block in zip(early, done):
        half[d] = block
    (rest,) = second_step(me, later.reshape(32, 2, slices * 16, 256), turned, False)
    rest = exchange(rest.reshape(64, 32, 128), ("z",) + CUTS)
    sums = list(total_step(me, half))
    for dy in range(1, RING):
        sums[dy] = lax.ppermute(sums[dy], "y", [(y, y ^ dy) for y in range(RING)])
    across = lax.ppermute(pick_step(sums), "xh", [(0, 1), (1, 0)])
    return lay_step(me, rest.reshape(DEPTH, 8, 32, 128), across, sums)


def solution(mesh):
    fine = Mesh(mesh.devices.reshape(2, RING, DEPTH, 2, 2), ("xh", "y", "z", "xl", "core"))
    in_specs = (
        P(None, CUTS, MODE, None, None, None),
        P(None, CUTS, None, None),
        P(None, CUTS, MODE, None),
    )
    return jax.shard_map(
        shards, mesh=fine, in_specs=in_specs, out_specs=P(None, CUTS, MODE, None), check_vma=False
    )
```

```python
import functools

import jax
import jax.numpy as jnp
from jax import lax
from jax.experimental import pallas as pl
from jax.experimental.pallas import tpu as pltpu
from jax.sharding import Mesh
from jax.sharding import PartitionSpec as P

PLANE = ("xh", "y", "xl", "core")
CUTS = ("xh", "y")
MODE = ("z", "xl", "core")
ROWS = ("xh", "xl")
NT = (((1,), (1,)), ((), ()))
NN = (((1,), (0,)), ((), ()))
RING = 4
DEPTH = 8
ANY = pl.BlockSpec(memory_space=pl.ANY)
VMEM = pl.BlockSpec(memory_space=pltpu.VMEM)
SMEM = pl.BlockSpec(memory_space=pltpu.SMEM)


def first_kernel(lh, stem_hbm, branch_hbm, out_hbm, stem, branch, lhs, out, in_sem, branch_sem, out_sem):
    count = stem.shape[1] // 2
    parts = [pl.ds(h * count, count) for h in range(2)]
    stem_copies, branch_copies, sends = [], [], []
    for h, part in enumerate(parts):
        branch_copies.append(pltpu.make_async_copy(branch_hbm.at[:, part], branch.at[:, part], branch_sem.at[h]))
        stem_copies.append(pltpu.make_async_copy(stem_hbm.at[:, part], stem.at[:, part], in_sem.at[h]))
        branch_copies[h].start()
        stem_copies[h].start()
    row = lax.broadcasted_iota(jnp.int32, (128, 256), 0)
    col = lax.broadcasted_iota(jnp.int32, (128, 256), 1)
    regroup = (col == (row % 16) * 16 + row // 16 * 2 + lh).astype(jnp.bfloat16)
    for h, part in enumerate(parts):
        branch_copies[h].wait()
        for s in range(h * count, (h + 1) * count):
            br = [
                lax.dot_general(regroup, branch[r, s], NT, preferred_element_type=jnp.float32).astype(jnp.bfloat16)
                for r in range(2)
            ]
            lhs[s, 0:128, 0:256] = br[0]
            lhs[s, 0:128, 256:512] = -br[1]
            lhs[s, 128:256, 0:256] = br[1]
            lhs[s, 128:256, 256:512] = br[0]
        stem_copies[h].wait()
        for s in range(h * count, (h + 1) * count):
            for w in range(4):
                rhs = jnp.concatenate([stem[r, s, :, w].reshape(256, 256) for r in range(2)], axis=1)
                res = lax.dot_general(lhs[s], rhs, NT, preferred_element_type=jnp.float32).astype(jnp.bfloat16)
                for r in range(2):
                    out[:, w, r, s] = res[r * 128 : (r + 1) * 128].reshape(8, 16, 256)
        sends.append(pltpu.make_async_copy(out.at[:, :, :, part], out_hbm.at[:, :, :, part], out_sem.at[h]))
        sends[h].start()
    for send in sends:
        send.wait()


def first_step(stem, branch, lh, flops):
    slices = stem.shape[1]
    shape = (8, 4, 2, slices, 16, 256)
    return pl.pallas_call(
        functools.partial(first_kernel, lh),
        in_specs=[ANY] * 2,
        out_specs=ANY,
        out_shape=jax.ShapeDtypeStruct(shape, jnp.bfloat16),
        scratch_shapes=[
            pltpu.VMEM(stem.shape, jnp.bfloat16),
            pltpu.VMEM(branch.shape, jnp.bfloat16),
            pltpu.VMEM((slices, 256, 512), jnp.bfloat16),
            pltpu.VMEM(shape, jnp.bfloat16),
            pltpu.SemaphoreType.DMA((2,)),
            pltpu.SemaphoreType.DMA((2,)),
            pltpu.SemaphoreType.DMA((2,)),
        ],
        compiler_params=pltpu.CompilerParams(vmem_limit_bytes=56 << 20),
        cost_estimate=pl.CostEstimate(flops=flops, bytes_accessed=7 << 20, transcendentals=0),
        name="first_step",
    )(stem, branch)


def turn_kernel(me_ref, *refs):
    own, other, out_ref = refs[:RING], refs[RING:-1], refs[-1]
    first_core = me_ref[2] == 0
    for dx in range(RING):
        x = me_ref[0] ^ dx
        for dy in range(RING):
            y = me_ref[1] ^ dy
            at = pl.multiple_of((((x // 2) * RING + y) * 2 + x % 2) * 128, 128)
            for r in range(2):
                low = jnp.where(first_core, own[dx][dy, r], other[dx][dy, r])
                high = jnp.where(first_core, other[dy][dx, r], own[dy][dx, r])
                out_ref[r, :, pl.ds(at, 128)] = jnp.concatenate([low, high], axis=0).T


def turn_step(me, own, other):
    return pl.pallas_call(
        turn_kernel,
        in_specs=[SMEM] + [VMEM] * (2 * RING),
        out_specs=VMEM,
        out_shape=jax.ShapeDtypeStruct((2, 512, 2048), jnp.bfloat16),
        compiler_params=pltpu.CompilerParams(vmem_limit_bytes=24 << 20),
        cost_estimate=pl.CostEstimate(flops=10000000000, bytes_accessed=8 << 20, transcendentals=0),
        name="turn_step",
    )(me, *own, *other)


def second_kernel(split, me_ref, x_hbm, b_hbm, *refs):
    if split:
        x, b, (out, out_sem), out_hbm = x_hbm, b_hbm, refs[-2:], refs[:-2]
    else:
        x, b, x_sem, b_sem, out, out_sem = refs[-6:]
        out_hbm = refs[:-6]
        x_copy = pltpu.make_async_copy(x_hbm, x, x_sem)
        b_copies = [
            pltpu.make_async_copy(b_hbm.at[:, pl.ds(h * 256, 256)], b.at[:, pl.ds(h * 256, 256)], b_sem.at[h])
            for h in range(2)
        ]
        for copy in (x_copy, *b_copies):
            copy.start()

    def dot(left, right):
        return lax.dot_general(left, right, NN, preferred_element_type=jnp.float32)

    if not split:
        x_copy.wait()
    xr, xi = (x[:, r].reshape(2048, 256) for r in range(2))
    sends = []
    for t in range(4):
        if t % 2 == 0 and not split:
            b_copies[t // 2].wait()
        rows = slice(t * 128, (t + 1) * 128)
        br, bi = b[0, rows], b[1, rows]
        res = [dot(br, xr) + dot(-bi, xi), dot(bi, xr) + dot(br, xi)]
        res = [part.astype(jnp.bfloat16) for part in res]
        for q in range(2):
            parts = [res[r][q * 64 + jh * 32 : q * 64 + (jh + 1) * 32] for jh in range(2) for r in range(2)]
            for za in range(DEPTH):
                out[za, t * 2 + q] = jnp.concatenate([part[:, za * 32 : (za + 1) * 32] for part in parts], axis=1)
        if t % 2 == 1 and not split:
            part = pl.ds(t * 2 - 2, 4)
            sends.append(pltpu.make_async_copy(out.at[:, part], out_hbm[0].at[:, part], out_sem.at[t // 2]))
            sends[-1].start()
    if split:
        for d in range(DEPTH):
            sends.append(pltpu.make_async_copy(out.at[me_ref[3] ^ d], out_hbm[d], out_sem.at[d]))
            sends[-1].start()
    for send in sends:
        send.wait()


def second_step(me, x, b2, split):
    shape = (DEPTH, 8, 32, 128)
    if split:
        out_shape = [jax.ShapeDtypeStruct(shape[1:], jnp.bfloat16)] * DEPTH
    else:
        out_shape = [jax.ShapeDtypeStruct(shape, jnp.bfloat16)]
    held = [] if split else [
        pltpu.VMEM((32, 2, 64, 256), jnp.bfloat16),
        pltpu.VMEM((2, 512, 2048), jnp.bfloat16),
        pltpu.SemaphoreType.DMA,
        pltpu.SemaphoreType.DMA((2,)),
    ]
    return pl.pallas_call(
        functools.partial(second_kernel, split),
        in_specs=[SMEM] + [VMEM if split else ANY] * 2,
        out_specs=[ANY] * len(out_shape),
        out_shape=out_shape,
        scratch_shapes=held + [pltpu.VMEM(shape, jnp.bfloat16), pltpu.SemaphoreType.DMA((DEPTH,))],
        compiler_params=pltpu.CompilerParams(vmem_limit_bytes=(24 if split else 60) << 20),
        cost_estimate=pl.CostEstimate(flops=2150000000, bytes_accessed=7 << 20, transcendentals=0),
        name="second_step",
    )(me, x, b2)


def total_kernel(me_ref, *refs):
    blocks, outs, sums = refs[:DEPTH], refs[DEPTH:-1], refs[-1]
    acc = blocks[0][...].astype(jnp.float32)
    for block in blocks[1:]:
        acc = acc + block[...].astype(jnp.float32)
    sums[...] = acc
    for dy in range(RING):
        for dx in range(2):
            outs[dy][dx] = sums[(me_ref[0] // 2 ^ dx) * RING + (me_ref[1] ^ dy)]


def total_step(me, blocks):
    return pl.pallas_call(
        total_kernel,
        in_specs=[SMEM] + [VMEM] * DEPTH,
        out_specs=[VMEM] * RING,
        out_shape=[jax.ShapeDtypeStruct((2, 32, 128), jnp.float32)] * RING,
        scratch_shapes=[pltpu.VMEM((8, 32, 128), jnp.float32)],
        compiler_params=pltpu.CompilerParams(vmem_limit_bytes=16 << 20),
        cost_estimate=pl.CostEstimate(flops=10000000000, bytes_accessed=1 << 20, transcendentals=0),
        name="total_step",
    )(me, *blocks)


def pick_kernel(*refs):
    for n, ref in enumerate(refs[:-1]):
        refs[-1][n] = ref[1]


def pick_step(sums):
    return pl.pallas_call(
        pick_kernel,
        in_specs=[VMEM] * RING,
        out_specs=VMEM,
        out_shape=jax.ShapeDtypeStruct((RING, 32, 128), jnp.float32),
        compiler_params=pltpu.CompilerParams(vmem_limit_bytes=16 << 20),
        cost_estimate=pl.CostEstimate(flops=1000000, bytes_accessed=1 << 17, transcendentals=0),
        name="pick_step",
    )(*sums)


def lay_kernel(me_ref, later_ref, across_ref, *refs):
    out_hbm, held, out, out_sem = refs[-4:]
    xh = me_ref[0] // 2
    for dy in range(RING):
        held[xh * RING + (me_ref[1] ^ dy)] = refs[dy][0]
        held[(1 - xh) * RING + (me_ref[1] ^ dy)] = across_ref[dy]
    sums = []
    for i in range(8):
        acc = later_ref[0, i].astype(jnp.float32)
        for z in range(1, DEPTH):
            acc = acc + later_ref[z, i].astype(jnp.float32)
        sums.append((held[i], acc))
    sends = []
    for r in range(2):
        for jh in range(2):
            at = jh * 64 + r * 32
            out[r, jh * 32 : (jh + 1) * 32, 0] = jnp.concatenate(
                [half[:, at : at + 32] for pair in sums for half in pair], axis=1
            )
        sends.append(pltpu.make_async_copy(out.at[r], out_hbm.at[r], out_sem.at[r]))
        sends[r].start()
    for send in sends:
        send.wait()


def lay_step(me, later, across, sums):
    return pl.pallas_call(
        lay_kernel,
        in_specs=[SMEM] + [VMEM] * (2 + RING),
        out_specs=ANY,
        out_shape=jax.ShapeDtypeStruct((2, 64, 1, 512), jnp.float32),
        scratch_shapes=[
            pltpu.VMEM((8, 32, 128), jnp.float32),
            pltpu.VMEM((2, 64, 1, 512), jnp.float32),
            pltpu.SemaphoreType.DMA((2,)),
        ],
        compiler_params=pltpu.CompilerParams(vmem_limit_bytes=16 << 20),
        cost_estimate=pl.CostEstimate(flops=1000000, bytes_accessed=1 << 20, transcendentals=0),
        name="lay_step",
    )(me, later, across, *sums)


def place(x, y, core):
    return ((x // 2 * RING + y) * 2 + x % 2) * 2 + core


def ring_blocks(block, stage):
    blocks = [block]
    for d in range(1, RING):
        pairs = []
        for x in range(RING):
            for y in range(RING):
                for core in range(2):
                    along_y = core == stage
                    source = place(x, y ^ d, core) if along_y else place(x ^ d, y, core)
                    pairs.append((source, place(x, y, core)))
        blocks.append(lax.ppermute(block, PLANE, pairs))
    return blocks


def pack_kernel(*refs):
    rows = refs[0].shape[0]
    for n, ref in enumerate(refs[:-1]):
        refs[-1][n * rows : (n + 1) * rows] = ref[...]


def pack(blocks):
    return pl.pallas_call(
        pack_kernel,
        in_specs=[VMEM] * len(blocks),
        out_specs=VMEM,
        out_shape=jax.ShapeDtypeStruct((len(blocks) * blocks[0].shape[0], *blocks[0].shape[1:]), blocks[0].dtype),
        compiler_params=pltpu.CompilerParams(vmem_limit_bytes=24 << 20),
        cost_estimate=pl.CostEstimate(flops=1000000, bytes_accessed=1 << 20, transcendentals=0),
        name="pack",
    )(*blocks)


def exchange(block, axes):
    return lax.all_to_all(block, axes, split_axis=0, concat_axis=0, tiled=True)


def shards(stem_tensor, branch_first, branch_second):
    slices = stem_tensor.shape[1]
    me = [lax.axis_index(axis) for axis in (ROWS, "y", "core", "z")]
    me = jnp.stack(me).astype(jnp.int32)
    stem = stem_tensor.reshape(2, slices, 8, 4, 32, 256)
    near = ring_blocks(branch_second.reshape(1, 2, slices * 16, 512), 0)
    sent = first_step(stem, branch_first, 0, 1200000000)
    sent, near, stem = lax.optimization_barrier((sent, near, stem))
    own = ring_blocks(pack(near), 1)
    arrived = exchange(sent.reshape(32, 2 * slices * 16, 256), PLANE)
    later = first_step(stem, branch_first, 1, 1000000)
    other = [lax.ppermute(block, "core", [(0, 1), (1, 0)]) for block in own]
    blocks = (RING, 2, slices * 16, 512)
    own, other = ([block.reshape(blocks) for block in part] for part in (own, other))
    turned = turn_step(me, own, other)
    arrived, later, me = lax.optimization_barrier((arrived, later, me))
    later = exchange(later.reshape(32, 2 * slices * 16, 256), PLANE)
    half = list(second_step(me, arrived.reshape(32, 2, slices * 16, 256), turned, True))
    for d in range(1, DEPTH):
        half[d] = lax.ppermute(half[d], "z", [(z, z ^ d) for z in range(DEPTH)])
    early = (0, 1, 2, 3)
    later, *done = lax.optimization_barrier((later, *[half[d] for d in early]))
    for d, block in zip(early, done):
        half[d] = block
    (rest,) = second_step(me, later.reshape(32, 2, slices * 16, 256), turned, False)
    rest = exchange(rest.reshape(64, 32, 128), ("z",) + CUTS)
    sums = list(total_step(me, half))
    for dy in range(1, RING):
        sums[dy] = lax.ppermute(sums[dy], "y", [(y, y ^ dy) for y in range(RING)])
    across = lax.ppermute(pick_step(sums), "xh", [(0, 1), (1, 0)])
    return lay_step(me, rest.reshape(DEPTH, 8, 32, 128), across, sums)


def solution(mesh):
    fine = Mesh(mesh.devices.reshape(2, RING, DEPTH, 2, 2), ("xh", "y", "z", "xl", "core"))
    in_specs = (
        P(None, CUTS, MODE, None, None, None),
        P(None, CUTS, None, None),
        P(None, CUTS, MODE, None),
    )
    return jax.shard_map(
        shards, mesh=fine, in_specs=in_specs, out_specs=P(None, CUTS, MODE, None), check_vma=False
    )
```

```python
import functools

import jax
import jax.numpy as jnp
from jax import lax
from jax.experimental import pallas as pl
from jax.experimental.pallas import tpu as pltpu
from jax.sharding import Mesh
from jax.sharding import PartitionSpec as P

PLANE = ("xh", "y", "xl", "core")
CUTS = ("xh", "y")
MODE = ("z", "xl", "core")
ROWS = ("xh", "xl")
NT = (((1,), (1,)), ((), ()))
NN = (((1,), (0,)), ((), ()))
RING = 4
DEPTH = 8
ANY = pl.BlockSpec(memory_space=pl.ANY)
VMEM = pl.BlockSpec(memory_space=pltpu.VMEM)
SMEM = pl.BlockSpec(memory_space=pltpu.SMEM)


def first_kernel(lh, stem_hbm, branch_hbm, out_hbm, stem, branch, lhs, out, in_sem, branch_sem, out_sem):
    slices = stem.shape[1]
    stem_copies, branch_copies, sends = [], [], []
    for s in range(slices):
        branch_copies.append(pltpu.make_async_copy(branch_hbm.at[:, s], branch.at[:, s], branch_sem.at[s]))
        stem_copies.append(pltpu.make_async_copy(stem_hbm.at[:, s], stem.at[:, s], in_sem.at[s]))
        branch_copies[s].start()
        stem_copies[s].start()
    row = lax.broadcasted_iota(jnp.int32, (128, 256), 0)
    col = lax.broadcasted_iota(jnp.int32, (128, 256), 1)
    regroup = (col == (row % 16) * 16 + row // 16 * 2 + lh).astype(jnp.bfloat16)
    for s in range(slices):
        branch_copies[s].wait()
        br = [
            lax.dot_general(regroup, branch[r, s], NT, preferred_element_type=jnp.float32).astype(jnp.bfloat16)
            for r in range(2)
        ]
        lhs[s, 0:128, 0:256] = br[0]
        lhs[s, 0:128, 256:512] = -br[1]
        lhs[s, 128:256, 0:256] = br[1]
        lhs[s, 128:256, 256:512] = br[0]
        stem_copies[s].wait()
        for w in range(4):
            rhs = jnp.concatenate([stem[r, s, :, w].reshape(256, 256) for r in range(2)], axis=1)
            res = lax.dot_general(lhs[s], rhs, NT, preferred_element_type=jnp.float32).astype(jnp.bfloat16)
            for r in range(2):
                out[:, w, r, s] = res[r * 128 : (r + 1) * 128].reshape(8, 16, 256)
        sends.append(pltpu.make_async_copy(out.at[:, :, :, s], out_hbm.at[:, :, :, s], out_sem.at[s]))
        sends[s].start()
    for send in sends:
        send.wait()


def first_step(stem, branch, lh, flops):
    slices = stem.shape[1]
    shape = (8, 4, 2, slices, 16, 256)
    return pl.pallas_call(
        functools.partial(first_kernel, lh),
        in_specs=[ANY] * 2,
        out_specs=ANY,
        out_shape=jax.ShapeDtypeStruct(shape, jnp.bfloat16),
        scratch_shapes=[
            pltpu.VMEM(stem.shape, jnp.bfloat16),
            pltpu.VMEM(branch.shape, jnp.bfloat16),
            pltpu.VMEM((slices, 256, 512), jnp.bfloat16),
            pltpu.VMEM(shape, jnp.bfloat16),
            pltpu.SemaphoreType.DMA((slices,)),
            pltpu.SemaphoreType.DMA((slices,)),
            pltpu.SemaphoreType.DMA((slices,)),
        ],
        compiler_params=pltpu.CompilerParams(vmem_limit_bytes=56 << 20),
        cost_estimate=pl.CostEstimate(flops=flops, bytes_accessed=7 << 20, transcendentals=0),
        name="first_step",
    )(stem, branch)


def turn_kernel(me_ref, *refs):
    own, other, out_ref = refs[:RING], refs[RING:-1], refs[-1]
    first_core = me_ref[2] == 0
    for dx in range(RING):
        x = me_ref[0] ^ dx
        for dy in range(RING):
            y = me_ref[1] ^ dy
            at = pl.multiple_of((((x // 2) * RING + y) * 2 + x % 2) * 128, 128)
            for r in range(2):
                low = jnp.where(first_core, own[dx][dy, r], other[dx][dy, r])
                high = jnp.where(first_core, other[dy][dx, r], own[dy][dx, r])
                out_ref[r, :, pl.ds(at, 128)] = jnp.concatenate([low, high], axis=0).T


def turn_step(me, own, other):
    return pl.pallas_call(
        turn_kernel,
        in_specs=[SMEM] + [VMEM] * (2 * RING),
        out_specs=VMEM,
        out_shape=jax.ShapeDtypeStruct((2, 512, 2048), jnp.bfloat16),
        compiler_params=pltpu.CompilerParams(vmem_limit_bytes=24 << 20),
        cost_estimate=pl.CostEstimate(flops=10000000000, bytes_accessed=8 << 20, transcendentals=0),
        name="turn_step",
    )(me, *own, *other)


def second_kernel(split, me_ref, x_hbm, b_hbm, *refs):
    x, b, out, x_sem, b_sem, out_sem = refs[-6:]
    out_hbm = refs[:-6]
    x_copy = pltpu.make_async_copy(x_hbm, x, x_sem)
    b_copies = [
        pltpu.make_async_copy(b_hbm.at[:, pl.ds(h * 256, 256)], b.at[:, pl.ds(h * 256, 256)], b_sem.at[h])
        for h in range(2)
    ]
    for copy in (x_copy, *b_copies):
        copy.start()

    def dot(left, right):
        return lax.dot_general(left, right, NN, preferred_element_type=jnp.float32)

    x_copy.wait()
    xr, xi = (x[:, r].reshape(2048, 256) for r in range(2))
    sends = []
    for t in range(4):
        if t % 2 == 0:
            b_copies[t // 2].wait()
        rows = slice(t * 128, (t + 1) * 128)
        br, bi = b[0, rows], b[1, rows]
        res = [dot(br, xr) + dot(-bi, xi), dot(bi, xr) + dot(br, xi)]
        res = [part.astype(jnp.bfloat16) for part in res]
        for q in range(2):
            parts = [res[r][q * 64 + jh * 32 : q * 64 + (jh + 1) * 32] for jh in range(2) for r in range(2)]
            for za in range(DEPTH):
                at = (za, t * 2 + q) if split else (t * 2 + q, za)
                out[at] = jnp.concatenate([part[:, za * 32 : (za + 1) * 32] for part in parts], axis=1)
        if t % 2 == 1 and not split:
            part = pl.ds(t * 2 - 2, 4)
            sends.append(pltpu.make_async_copy(out.at[part], out_hbm[0].at[part], out_sem.at[t // 2]))
            sends[-1].start()
    if split:
        for d in range(DEPTH):
            sends.append(pltpu.make_async_copy(out.at[me_ref[3] ^ d], out_hbm[d], out_sem.at[d]))
            sends[-1].start()
    for send in sends:
        send.wait()


def second_step(me, x, b2, split):
    shape = (DEPTH, 8, 32, 128)
    if split:
        out_shape = [jax.ShapeDtypeStruct(shape[1:], jnp.bfloat16)] * DEPTH
    else:
        out_shape = [jax.ShapeDtypeStruct(shape, jnp.bfloat16)]
    return pl.pallas_call(
        functools.partial(second_kernel, split),
        in_specs=[SMEM, ANY, ANY],
        out_specs=[ANY] * len(out_shape),
        out_shape=out_shape,
        scratch_shapes=[
            pltpu.VMEM((32, 2, 64, 256), jnp.bfloat16),
            pltpu.VMEM((2, 512, 2048), jnp.bfloat16),
            pltpu.VMEM(shape, jnp.bfloat16),
            pltpu.SemaphoreType.DMA,
            pltpu.SemaphoreType.DMA((2,)),
            pltpu.SemaphoreType.DMA((DEPTH,)),
        ],
        compiler_params=pltpu.CompilerParams(vmem_limit_bytes=(24 if split else 60) << 20),
        cost_estimate=pl.CostEstimate(flops=2150000000, bytes_accessed=7 << 20, transcendentals=0),
        name="second_step",
    )(me, x, b2)


def total_kernel(me_ref, *refs):
    blocks, outs, sums = refs[:DEPTH], refs[DEPTH:-1], refs[-1]
    acc = blocks[0][...].astype(jnp.float32)
    for block in blocks[1:]:
        acc = acc + block[...].astype(jnp.float32)
    sums[...] = acc
    for dy in range(RING):
        for dx in range(2):
            outs[dy][dx] = sums[(me_ref[0] // 2 ^ dx) * RING + (me_ref[1] ^ dy)]


def total_step(me, blocks):
    return pl.pallas_call(
        total_kernel,
        in_specs=[SMEM] + [VMEM] * DEPTH,
        out_specs=[VMEM] * RING,
        out_shape=[jax.ShapeDtypeStruct((2, 32, 128), jnp.float32)] * RING,
        scratch_shapes=[pltpu.VMEM((8, 32, 128), jnp.float32)],
        compiler_params=pltpu.CompilerParams(vmem_limit_bytes=16 << 20),
        cost_estimate=pl.CostEstimate(flops=10000000000, bytes_accessed=1 << 20, transcendentals=0),
        name="total_step",
    )(me, *blocks)


def pick_kernel(*refs):
    for n, ref in enumerate(refs[:-1]):
        refs[-1][n] = ref[1]


def pick_step(sums):
    return pl.pallas_call(
        pick_kernel,
        in_specs=[VMEM] * RING,
        out_specs=VMEM,
        out_shape=jax.ShapeDtypeStruct((RING, 32, 128), jnp.float32),
        compiler_params=pltpu.CompilerParams(vmem_limit_bytes=16 << 20),
        cost_estimate=pl.CostEstimate(flops=1000000, bytes_accessed=1 << 17, transcendentals=0),
        name="pick_step",
    )(*sums)


def lay_kernel(me_ref, later_ref, across_ref, *refs):
    out_ref, held = refs[-2:]
    xh = me_ref[0] // 2
    for dy in range(RING):
        held[xh * RING + (me_ref[1] ^ dy)] = refs[dy][0]
        held[(1 - xh) * RING + (me_ref[1] ^ dy)] = across_ref[dy]
    sums = []
    for i in range(8):
        acc = later_ref[i, 0].astype(jnp.float32)
        for z in range(1, DEPTH):
            acc = acc + later_ref[i, z].astype(jnp.float32)
        sums.append((held[i], acc))
    for r in range(2):
        for jh in range(2):
            at = jh * 64 + r * 32
            out_ref[r, jh * 32 : (jh + 1) * 32, 0] = jnp.concatenate(
                [half[:, at : at + 32] for pair in sums for half in pair], axis=1
            )


def lay_step(me, later, across, sums):
    return pl.pallas_call(
        lay_kernel,
        in_specs=[SMEM] + [VMEM] * (2 + RING),
        out_specs=VMEM,
        out_shape=jax.ShapeDtypeStruct((2, 64, 1, 512), jnp.float32),
        scratch_shapes=[pltpu.VMEM((8, 32, 128), jnp.float32)],
        compiler_params=pltpu.CompilerParams(vmem_limit_bytes=16 << 20),
        cost_estimate=pl.CostEstimate(flops=1000000, bytes_accessed=1 << 20, transcendentals=0),
        name="lay_step",
    )(me, later, across, *sums)


def place(x, y, core):
    return ((x // 2 * RING + y) * 2 + x % 2) * 2 + core


def ring_blocks(block, stage):
    blocks = [block]
    for d in range(1, RING):
        pairs = []
        for x in range(RING):
            for y in range(RING):
                for core in range(2):
                    along_y = core == stage
                    source = place(x, y ^ d, core) if along_y else place(x ^ d, y, core)
                    pairs.append((source, place(x, y, core)))
        blocks.append(lax.ppermute(block, PLANE, pairs))
    return blocks


def pack_kernel(*refs):
    rows = refs[0].shape[0]
    for n, ref in enumerate(refs[:-1]):
        refs[-1][n * rows : (n + 1) * rows] = ref[...]


def pack(blocks):
    return pl.pallas_call(
        pack_kernel,
        in_specs=[VMEM] * len(blocks),
        out_specs=VMEM,
        out_shape=jax.ShapeDtypeStruct((len(blocks) * blocks[0].shape[0], *blocks[0].shape[1:]), blocks[0].dtype),
        compiler_params=pltpu.CompilerParams(vmem_limit_bytes=24 << 20),
        cost_estimate=pl.CostEstimate(flops=1000000, bytes_accessed=1 << 20, transcendentals=0),
        name="pack",
    )(*blocks)


def exchange(block, axes):
    return lax.all_to_all(block, axes, split_axis=0, concat_axis=0, tiled=True)


def shards(stem_tensor, branch_first, branch_second):
    slices = stem_tensor.shape[1]
    me = [lax.axis_index(axis) for axis in (ROWS, "y", "core", "z")]
    me = jnp.stack(me).astype(jnp.int32)
    stem = stem_tensor.reshape(2, slices, 8, 4, 32, 256)
    near = ring_blocks(branch_second.reshape(1, 2, slices * 16, 512), 0)
    sent = first_step(stem, branch_first, 0, 1200000000)
    sent, near, stem = lax.optimization_barrier((sent, near, stem))
    own = ring_blocks(pack(near), 1)
    arrived = exchange(sent.reshape(32, 2 * slices * 16, 256), PLANE)
    later = first_step(stem, branch_first, 1, 1000000)
    other = [lax.ppermute(block, "core", [(0, 1), (1, 0)]) for block in own]
    blocks = (RING, 2, slices * 16, 512)
    own, other = ([block.reshape(blocks) for block in part] for part in (own, other))
    turned = turn_step(me, own, other)
    arrived, later = lax.optimization_barrier((arrived, later))
    later = exchange(later.reshape(32, 2 * slices * 16, 256), PLANE)
    half = list(second_step(me, arrived.reshape(32, 2, slices * 16, 256), turned, True))
    for d in range(1, DEPTH):
        half[d] = lax.ppermute(half[d], "z", [(z, z ^ d) for z in range(DEPTH)])
    early = (0, 1, 2, 3)
    later, *done = lax.optimization_barrier((later, *[half[d] for d in early]))
    for d, block in zip(early, done):
        half[d] = block
    (rest,) = second_step(me, later.reshape(32, 2, slices * 16, 256), turned, False)
    rest = exchange(rest.reshape(64, 32, 128), CUTS + ("z",))
    sums = list(total_step(me, half))
    for dy in range(1, RING):
        sums[dy] = lax.ppermute(sums[dy], "y", [(y, y ^ dy) for y in range(RING)])
    across = lax.ppermute(pick_step(sums), "xh", [(0, 1), (1, 0)])
    return lay_step(me, rest.reshape(DEPTH, 8, 32, 128), across, sums)


def solution(mesh):
    fine = Mesh(mesh.devices.reshape(2, RING, DEPTH, 2, 2), ("xh", "y", "z", "xl", "core"))
    in_specs = (
        P(None, CUTS, MODE, None, None, None),
        P(None, CUTS, None, None),
        P(None, CUTS, MODE, None),
    )
    return jax.shard_map(
        shards, mesh=fine, in_specs=in_specs, out_specs=P(None, CUTS, MODE, None), check_vma=False
    )
```
